256 devices in a mesh: seq: 16 (over x_hi, z), dp: 4 (over x_lo, core), tensor: 4 (over y).
Axes of the slice: x: 4 (x_hi: 2, x_lo: 2; x = x_hi * 2 + x_lo), y: 4, z: 8, core: 2. Of those that a mesh axis runs over, the one named last changes fastest.
Arguments:
- layer_input: bfloat16 [4, 8192, 512], P('dp', 'seq'), may hold values from -6 to 6
- grad_output: bfloat16 [4, 8192, 512], P('dp', 'seq'), may hold values from -6 to 6
- weight_in: bfloat16 [512, 2048], P(None, 'tensor'), may hold values from -0.25 to 0.25
- weight_out: bfloat16 [512, 512], P('tensor'), may hold values from -0.25 to 0.25
- time_table: float32 [4, 128], P('tensor'), may hold values from -1 to 1
- user_lengths: int32 [4, 3], P('dp'), may hold values from 1 to 32, 64 in all within a row
- time_buckets: int32 [4, 8192], P('dp', 'seq'), may hold values from 0 to 127
Outputs:
- grad_input: bfloat16 [4, 8192, 512], P('dp', 'seq', 'tensor')
- grad_weight_in: float32 [512, 2048], P(None, 'tensor')
- grad_weight_out: float32 [512, 512], P('tensor')
The draws below stay inside these ranges and needn't reach their ends.
Inputs may be any that keep to these rules, and one draw needn't show every extreme that they name: user_lengths[w, 0] and user_lengths[w, 1] are the two users' lengths in blocks of 128 rows, user_lengths[w, 2] the padding at the window's end; each row sums to 64.
All inputs are finite; a program needn't handle non-finite values.
Results may differ from the reference program's by a relative error of at most 0.015.
Values may be sent and summed in bfloat16 or wider, within the bound.
No kernel may reach another device: no remote copies, remote signals or barrier semaphores. Data moves between devices by JAX's collectives and lax.ppermute only.
A program may use at most 64 MiB of HBM per device.

```python
import math
import jax
import jax.numpy as jnp
import numpy as np
from jax import lax

D = 512
HEADS = 4
DH = 128
NB = 128
PAD_ROWS = 128
TOK_DEV = 512
LEN = 8192
WINDOWS = 4
N_SEQ = 16


def set_ends(drawn, rng, smallest, largest):
    longest = drawn.shape.index(max(drawn.shape))
    spots = []
    for shift in (0, 1):
        where = [jax.random.randint(jax.random.fold_in(rng, axis), (), 0, length) for axis, length in enumerate(drawn.shape)]
        where[longest] = (where[longest] + shift) % drawn.shape[longest]
        spots.append(tuple(where))
    return drawn.at[spots[0]].set(smallest).at[spots[1]].set(largest)


def steps_of(rng, extent, split, smallest, top_value):
    def one(dim, parts):
        heights = jax.random.uniform(jax.random.fold_in(jax.random.fold_in(rng, 6), dim), (parts,), jnp.float32, smallest / len(split), top_value / len(split))
        return jnp.repeat(jnp.exp(heights), extent[dim] // parts).reshape((-1,) + (1,) * (len(extent) - dim - 1))

    level = one(*split[0])
    for cut in split[1:]:
        level = level * one(*cut)
    return level


def split_up(number_of, total, bound, lean):
    portions = [(1 << 20) // math.isqrt(rank ** lean) + 1 for rank in range(2, number_of + 1)]
    spare, given = total - bound - (number_of - 1), [1] * (number_of - 1)
    while spare > 0:
        movable = [i for i in range(number_of - 1) if given[i] < bound]
        mass, remaining = sum([portions[i] for i in movable]), spare
        for i in movable:
            more = min(bound - given[i], max(1, remaining * portions[i] // mass), spare)
            given[i] = given[i] + more
            spare = spare - more
    return np.array([bound] + given)


def uneven(own_key, amount, total, limit, skew):
    if amount == 2:
        one = jax.random.randint(own_key, (), max(1, total - limit), min(limit, total - 1) + 1)
        return jnp.stack([one, total - one])
    tallies = jnp.asarray(split_up(amount, total, limit, skew), jnp.int32)
    pairs = (amount - 1) // 2
    source_of, sink = tallies[1:1 + 2 * pairs:2], tallies[2:2 + 2 * pairs:2]
    room = jnp.minimum(source_of - 1, limit - sink)
    passed = jax.random.randint(jax.random.fold_in(own_key, 1), (pairs,), 0, 1 << 20) % (room + 1)
    tallies = tallies.at[1:1 + 2 * pairs:2].set(source_of - passed).at[2:2 + 2 * pairs:2].set(sink + passed)
    return tallies[jax.random.permutation(jax.random.fold_in(own_key, 2), amount)]


def noise(own_key, dims, scale, most, shards=(), held_as=jnp.bfloat16):
    factor_of = steps_of(own_key, dims, shards, -0.22, 0.18) if shards else 1.0
    values = jax.random.normal(own_key, dims, jnp.float32) * scale * factor_of
    return jnp.minimum(jnp.maximum(values, -most), most).astype(held_as)


def setup_inputs(seed: int = 0) -> dict:
    key_of = jax.random.split(jax.random.key(seed), 8)
    layer_input = noise(key_of[0], (WINDOWS, LEN, D), 1.0, 6.0, ((0, 4), (1, 16)))
    grad_output = noise(key_of[1], (WINDOWS, LEN, D), 1.0, 6.0, ((0, 4), (1, 16)))
    weight_in = noise(key_of[2], (D, 4 * D), D ** -0.5, 0.25, ((1, 4),))
    weight_out = noise(key_of[3], (D, D), D ** -0.5, 0.25, ((0, 4),))
    time_table = jnp.clip(jax.random.uniform(key_of[4], (HEADS, NB), jnp.float32, -1.0, 1.0) * steps_of(key_of[4], (HEADS, NB), ((0, 4),), -0.4, 0.0), -1.0, 1.0)
    user_lengths = jax.vmap(lambda own: uneven(own, 3, LEN // PAD_ROWS, LEN // PAD_ROWS // 2, 0))(jax.random.split(key_of[5], WINDOWS)).reshape((WINDOWS, 3)).astype(jnp.int32)
    time_buckets = set_ends(jax.random.randint(key_of[6], (WINDOWS, LEN), 0, NB), jax.random.fold_in(key_of[6], 1), 0, NB - 1).astype(jnp.int32)
    return dict(layer_input=layer_input, grad_output=grad_output, weight_in=weight_in, weight_out=weight_out, time_table=time_table, user_lengths=user_lengths, time_buckets=time_buckets)


EPSILON = 0.05

def silu_slope(values):
    sigmoid = jax.nn.sigmoid(values)
    return sigmoid * (1.0 + values * (1.0 - sigmoid))

def time_position(rows, per_device, devices):
    half = per_device // 2
    device = rows // per_device
    offset = rows % per_device
    early = device * half + offset
    late = (2 * devices - 1 - device) * half + offset - half
    return jnp.where(offset < half, early, late).astype(jnp.int32)

def reference(layer_input, grad_output, weight_in, weight_out, time_table, user_lengths, time_buckets):
    factor = 1.0 / math.sqrt(DH)
    block = min(LEN, 512)
    blocks = LEN // block
    all_rows = jnp.arange(LEN, dtype=jnp.int32)
    positions = time_position(all_rows, TOK_DEV, N_SEQ)
    grad_inputs = []
    grad_win = jnp.zeros((D, 4 * D), jnp.float32)
    grad_wout = jnp.zeros((D, D), jnp.float32)
    for window in range(WINDOWS):
        inputs_here = layer_input[window]
        upstream = grad_output[window]
        first_end = (PAD_ROWS * user_lengths[window, 0]).astype(jnp.int32)
        second_end = (first_end + PAD_ROWS * user_lengths[window, 1]).astype(jnp.int32)
        user_ids = (positions >= first_end).astype(jnp.int32) + (positions >= second_end).astype(jnp.int32)
        zero_int = jnp.zeros_like(positions)
        user_first = jnp.where(positions < first_end, zero_int, jnp.where(positions < second_end, zero_int + first_end, zero_int + second_end))
        counts_all = jnp.maximum(positions - user_first + 1, 1).astype(jnp.float32)
        times = time_buckets[window]
        projected = jnp.dot(inputs_here, weight_in, preferred_element_type=jnp.float32)
        activated = jax.nn.silu(projected).astype(jnp.bfloat16)
        head_grads = []
        head_wout = []
        for head in range(HEADS):
            base = head * 4 * DH
            gate_part = activated[:, base:base + DH]
            value_part = activated[:, base + DH:base + 2 * DH]
            query_part = activated[:, base + 2 * DH:base + 3 * DH]
            key_part = activated[:, base + 3 * DH:base + 4 * DH]
            table_row = time_table[head]

            def tile(block_index):
                begin = (block_index * block).astype(jnp.int32)
                query_pos = lax.dynamic_slice_in_dim(positions, begin, block)
                query_blk = lax.dynamic_slice_in_dim(query_part, begin, block, 0)
                query_times = lax.dynamic_slice_in_dim(times, begin, block)
                query_users = lax.dynamic_slice_in_dim(user_ids, begin, block)
                counts = lax.dynamic_slice_in_dim(counts_all, begin, block)
                scores = jnp.dot(query_blk, key_part.T, preferred_element_type=jnp.float32) * factor
                scores = scores + jnp.take(table_row, jnp.abs(query_times[:, None] - times[None, :]))
                allowed = (positions[None, :] <= query_pos[:, None]) & (user_ids[None, :] == query_users[:, None]) & (query_pos < second_end)[:, None]
                attend = (jnp.where(allowed, jax.nn.silu(scores), 0.0) / counts[:, None]).astype(jnp.bfloat16)
                return (scores, allowed, counts, attend, begin)

            def forward_tile(block_index):
                unused_scores, unused_allowed, unused_counts, attend, unused_begin = tile(block_index)
                return jnp.dot(attend, value_part, preferred_element_type=jnp.float32)
            attended = lax.map(forward_tile, jnp.arange(blocks, dtype=jnp.int32)).reshape(LEN, DH)
            spread = jnp.sqrt(lax.optimization_barrier(jnp.mean(attended * attended, axis=-1, keepdims=True)) + EPSILON)
            normed = attended / spread
            gate_float = gate_part.astype(jnp.float32)
            gated = (normed * gate_float).astype(jnp.bfloat16)
            rows_out = weight_out[head * DH:(head + 1) * DH]
            grad_gated = jnp.dot(upstream, rows_out.T, preferred_element_type=jnp.float32)
            head_wout.append(jnp.dot(gated.T, upstream, preferred_element_type=jnp.float32))
            grad_gate = grad_gated * normed
            grad_normed = grad_gated * gate_float
            grad_attended = ((grad_normed - normed * lax.optimization_barrier(jnp.mean(grad_normed * normed, axis=-1, keepdims=True))) / spread).astype(jnp.bfloat16)

            def backward_tile(carry, block_index):
                grad_key, grad_value = carry
                scores, allowed, counts, attend, begin = tile(block_index)
                grad_blk = lax.dynamic_slice_in_dim(grad_attended, begin, block, 0)
                query_blk = lax.dynamic_slice_in_dim(query_part, begin, block, 0)
                raw = jnp.dot(grad_blk, value_part.T, preferred_element_type=jnp.float32)
                slope = (jnp.where(allowed, raw * silu_slope(scores), 0.0) / counts[:, None]).astype(jnp.bfloat16)
                grad_query_blk = jnp.dot(slope, key_part, preferred_element_type=jnp.float32) * factor
                grad_value = grad_value + jnp.dot(attend.T, grad_blk, preferred_element_type=jnp.float32)
                grad_key = grad_key + jnp.dot(slope.T, query_blk, preferred_element_type=jnp.float32)
                return ((grad_key, grad_value), grad_query_blk)
            zeros_head = jnp.zeros((LEN, DH), jnp.float32)
            (grad_key, grad_value), grad_query = lax.scan(backward_tile, (zeros_head, zeros_head), jnp.arange(blocks, dtype=jnp.int32))
            grad_query = grad_query.reshape(LEN, DH)
            grad_key = grad_key * factor
            head_grads.append(jnp.concatenate([grad_gate, grad_value, grad_query, grad_key], 1))
        grad_projected = (jnp.concatenate(head_grads, 1) * silu_slope(projected)).astype(jnp.bfloat16)
        grad_inputs.append(jnp.dot(grad_projected, weight_in.T, preferred_element_type=jnp.float32).astype(jnp.bfloat16))
        grad_win = grad_win + jnp.dot(inputs_here.T, grad_projected, preferred_element_type=jnp.float32)
        grad_wout = grad_wout + jnp.concatenate(head_wout, 0)
    normalizer = 1.0 / math.sqrt(WINDOWS * LEN)
    return (jnp.stack(grad_inputs, 0), grad_win * normalizer, grad_wout * normalizer)
```

```python
import functools
import math

import jax
import jax.numpy as jnp
from jax import lax
from jax.experimental import pallas as pl
from jax.experimental.pallas import tpu as pltpu
from jax.sharding import Mesh
from jax.sharding import PartitionSpec as P

PAD_ROWS = 128
EPSILON = 0.05
ROWS = 512
HALF = 256
DH = 128
NB = 128
WIDTH = 512
GROUP = 4
BIG = 1 << 24
BF = jnp.bfloat16
F32 = jnp.float32
FACTOR = 1.0 / math.sqrt(DH)
PIECE = 80
STEP = 2
LIST = 128

TRANSPOSED = ("z2", "z1", "xl", "core")
SWAP = [
    (8 * a + 4 * b + 2 * c + d, 8 * d + 4 * c + 2 * b + a)
    for a in (0, 1)
    for b in (0, 1)
    for c in (0, 1)
    for d in (0, 1)
]
FLIP = [(0, 1), (1, 0)]


def flip_x(rel):
    return [(i, i ^ rel) for i in range(4)]


def dot(a, b, dims=((1,), (0,))):
    return lax.dot_general(a, b, (dims, ((), ())), preferred_element_type=F32)


NT = ((1,), (1,))
TN = ((0,), (0,))


def call(kernel, outs, args, scratch=(), flops=0, unread=0, passed=0):
    specs = [pl.BlockSpec(memory_space=pltpu.VMEM)] * (len(args) - unread - passed)
    specs += [pl.BlockSpec(memory_space=pl.ANY)] * (unread + passed)
    for n, a in enumerate(args):
        if a.ndim == 1:
            specs[n] = pl.BlockSpec(memory_space=pltpu.SMEM)
    before = len(outs)
    outs = list(outs) + [(a.shape, a.dtype) for a in args[len(args) - passed :]]
    out_specs = [pl.BlockSpec(memory_space=pltpu.VMEM)] * before
    out_specs += [pl.BlockSpec(memory_space=pl.ANY)] * passed
    for n, (shape, _) in enumerate(outs):
        if len(shape) == 1:
            out_specs[n] = pl.BlockSpec(memory_space=pltpu.SMEM)
    moved = sum(a.size * a.dtype.itemsize for a in args)
    moved += sum(math.prod(s) * jnp.dtype(t).itemsize for s, t in outs)
    return pl.pallas_call(
        kernel,
        out_shape=[jax.ShapeDtypeStruct(s, t) for s, t in outs],
        in_specs=specs,
        out_specs=out_specs,
        input_output_aliases={len(args) - passed + n: before + n for n in range(passed)},
        scratch_shapes=list(scratch),
        compiler_params=pltpu.CompilerParams(vmem_limit_bytes=40 * 1024 * 1024),
        cost_estimate=pl.CostEstimate(flops=flops, bytes_accessed=moved, transcendentals=0),
    )(*args)


def prepare_kernel(x_ref, times_ref, lengths_ref, out_ref):
    out_ref[0:ROWS, :] = x_ref[...]
    row = lax.broadcasted_iota(jnp.int32, (16, WIDTH), 0)
    lengths = jnp.concatenate([lengths_ref[...]] * (WIDTH // DH), 1).astype(F32)
    times = times_ref[...].astype(F32)
    out_ref[ROWS:, :] = jnp.where(row == 0, times, jnp.where(row == 1, lengths, 0.0)).astype(BF)


def gated_kernel(upstream_ref, wout_ref, out_ref):
    out_ref[...] = dot(upstream_ref[...], wout_ref[...], NT).astype(BF)


def project_kernel(xa_ref, w_ref, table_ref, _, kv_ref, q_ref, gate_ref, slope_ref, __):
    projected = dot(xa_ref[0:ROWS, :], w_ref[...])
    sig = 0.5 + 0.5 * jnp.tanh(0.5 * projected)
    act = projected * sig
    slope_ref[...] = sig * (1.0 + projected * (1.0 - sig))
    gate_ref[...] = act[:, 0:DH].astype(BF)
    kv_ref[0:ROWS, DH : 2 * DH] = act[:, DH : 2 * DH].astype(BF)
    q_ref[:, 0:DH] = (act[:, 2 * DH : 3 * DH] * (0.5 * FACTOR)).astype(BF)
    kv_ref[0:ROWS, 0:DH] = act[:, 3 * DH : 4 * DH].astype(BF)
    times = xa_ref[ROWS : ROWS + 16, :].astype(F32)[0:1, :]
    row = lax.broadcasted_iota(jnp.int32, (16, HALF), 0)
    extra = jnp.where(row == 0, times[:, 0:HALF], jnp.where(row == 1, times[:, HALF:], 0.0))
    kv_ref[ROWS : ROWS + 16, :] = extra.astype(BF)
    table = jnp.broadcast_to(table_ref[...] * 0.5, (NB, NB))
    rolled = pltpu.roll(table, 0, 1, stride=1, stride_axis=0)
    first = lax.broadcasted_iota(jnp.int32, (NB, NB), 0)
    second = lax.broadcasted_iota(jnp.int32, (NB, NB), 1)
    square = jnp.where(second >= first, rolled, rolled.T).astype(BF)
    bucket = lax.broadcasted_iota(jnp.int32, (NB, ROWS), 0).astype(F32)
    hot = (bucket == times).astype(F32).astype(BF)
    q_ref[:, DH : 2 * DH] = dot(square, hot).T.astype(BF)


def first_of(rows, first_end, second_end):
    return jnp.where(rows < first_end, 0, jnp.where(rows < second_end, first_end, BIG))


def key_row_of(meta_ref, slot):
    x, core, z = (meta_ref[n] for n in range(2, 5))
    owner = x ^ (slot // 2)
    index = 8 * (owner // 2) + 2 * (owner % 2) + 4 * core + z
    return jnp.where(slot % 2 == 0, index, 31 - index) * HALF


def query_row_of(meta_ref, j):
    x, core, z = (meta_ref[n] for n in range(2, 5))
    rel = j % GROUP
    index = 8 * (x // 2) + 2 * (x % 2) + 4 * (core ^ (rel // 2)) + (z ^ (rel % 2))
    return jnp.where(j < GROUP, index, 31 - index) * HALF


def list_pairs(meta_ref, list_ref):
    first_end, second_end = meta_ref[0], meta_ref[1]

    def queries(j, count):
        row = query_row_of(meta_ref, j)
        lowest = first_of(row, first_end, second_end)

        def keys(slot, count):
            key_row = key_row_of(meta_ref, slot)
            valid = (key_row <= row) & (key_row + HALF > lowest)
            list_ref[count] = j * 8 + slot
            return count + valid.astype(jnp.int32)

        return lax.fori_loop(0, 2 * GROUP, keys, count, unroll=True)

    count = lax.fori_loop(0, 2 * GROUP, queries, jnp.int32(0))
    for more in range(STEP):
        list_ref[count + more] = -1
    list_ref[LIST - 1] = count


def sweep(meta_ref, list_ref, one, key_axis):
    def step(i, carry):
        done = []
        for n in range(STEP):
            item = list_ref[i * STEP + n]
            live = item >= 0
            item = jnp.maximum(item, 0)
            j, slot = item // 8, item % 8
            rows = jnp.where(live, query_row_of(meta_ref, j), -HALF)
            mask = mask_of(rows, key_row_of(meta_ref, slot), meta_ref[0], meta_ref[1], key_axis)
            done.append(one(j, slot, mask))
        for finish in done:
            finish()
        return carry

    lax.fori_loop(0, (list_ref[LIST - 1] + STEP - 1) // STEP, step, 0)


def mask_of(query_row, key_row, first_end, second_end, key_axis):
    shape_q = (HALF, 1) if key_axis == 1 else (1, HALF)
    rows_q = query_row + lax.broadcasted_iota(jnp.int32, shape_q, 1 - key_axis)
    rows_k = key_row + lax.broadcasted_iota(jnp.int32, (HALF, HALF), key_axis)
    return (rows_k <= rows_q) & (rows_k >= first_of(rows_q, first_end, second_end))


def forward_kernel(
    meta_ref, kv0, kv1, kv2, kv3, q0, q1, q2, q3, _,
    keep_ref, send_ref, k_ref, v_ref, q_ref, list_ref, acc,
):
    bucket = lax.broadcasted_iota(jnp.int32, (NB, HALF), 0).astype(F32)
    for rel, kv in enumerate((kv0, kv1, kv2, kv3)):
        tail = kv[ROWS : ROWS + 16, :].astype(F32)
        for half in (0, 1):
            rows = slice(half * HALF, (half + 1) * HALF)
            hot = (bucket == tail[half : half + 1, :]).astype(F32)
            k_ref[rel * 2 + half, :, 0:DH] = kv[rows, 0:DH]
            k_ref[rel * 2 + half, :, DH : 2 * DH] = hot.T.astype(BF)
            v_ref[rel * 2 + half] = kv[rows, DH : 2 * DH]
    for rel, q in enumerate((q0, q1, q2, q3)):
        for half in (0, 1):
            q_ref[half * GROUP + rel] = q[half * HALF : (half + 1) * HALF, :]
    acc[...] = jnp.zeros_like(acc)

    list_pairs(meta_ref, list_ref)

    def one(j, slot, mask):
        scores = dot(q_ref[j], k_ref[slot], NT)
        attend = jnp.where(mask, scores + scores * jnp.tanh(scores), 0.0)
        result = dot(attend.astype(BF), v_ref[slot])

        def finish():
            acc[j] += result

        return finish

    sweep(meta_ref, list_ref, one, 1)
    for rel in (0, 1):
        for half in (0, 1):
            rows = slice(rel * ROWS + half * HALF, rel * ROWS + (half + 1) * HALF)
            keep_ref[rows, :] = acc[half * GROUP + rel]
            send_ref[rows, :] = acc[half * GROUP + rel + 2].astype(BF)


def middle_kernel(
    meta_ref, keep, got_core, got_z, grad_gated_ref, gate, slope, grad_ref, gate_ref, gated_ref
):
    first_end, second_end, x, core, z = (meta_ref[n] for n in range(5))
    block = 8 * (x // 2) + 2 * (x % 2) + 4 * core + z
    offset = lax.broadcasted_iota(jnp.int32, (ROWS, 1), 0)
    rows = jnp.where(offset < HALF, block * HALF + offset, (31 - block) * HALF + offset - HALF)
    first = jnp.where(rows < first_end, 0, jnp.where(rows < second_end, first_end, second_end))
    inverse = 1.0 / jnp.maximum(rows - first + 1, 1).astype(F32)
    total = keep[0:ROWS, :] + got_core[0:ROWS, :].astype(F32) + got_z[...].astype(F32)
    attended = total * inverse
    spread = 1.0 / jnp.sqrt(jnp.mean(attended * attended, axis=-1, keepdims=True) + EPSILON)
    normed = attended * spread
    gate_float = gate[...].astype(F32)
    gated_ref[...] = (normed * gate_float).astype(BF)
    grad_gated = grad_gated_ref[...].astype(F32)
    gate_ref[...] = (grad_gated * normed * slope[:, 0:DH]).astype(BF)
    grad_normed = grad_gated * gate_float
    inner = jnp.mean(grad_normed * normed, axis=-1, keepdims=True)
    grad_ref[...] = ((grad_normed - normed * inner) * (spread * inverse * 0.5)).astype(BF)


def backward_kernel(
    meta_ref, list_ref, k_ref, v_ref, q_ref, g0, g1, g2, g3,
    own_ref, s1_ref, s2_ref, s3_ref, keep_ref, send_ref,
    grad, kt, acc_k, acc_v, acc_q,
):
    for rel, g in enumerate((g0, g1, g2, g3)):
        for half in (0, 1):
            grad[half * GROUP + rel] = g[half * HALF : (half + 1) * HALF, :]
    for slot in range(2 * GROUP):
        kt[slot] = k_ref[slot, :, 0:DH].astype(F32).T.astype(BF)
    acc_k[...] = jnp.zeros_like(acc_k)
    acc_v[...] = jnp.zeros_like(acc_v)
    acc_q[...] = jnp.zeros_like(acc_q)

    def one(j, slot, mask):
        scores = dot(k_ref[slot], q_ref[j], NT)
        raw = dot(v_ref[slot], grad[j], NT)
        tanh = jnp.tanh(scores)
        more = 1.0 + tanh
        attend = scores * more
        slope = jnp.where(mask, raw * (more + attend * (1.0 - tanh)), 0.0).astype(BF)
        attend = jnp.where(mask, attend, 0.0).astype(BF)
        grad_q = dot(kt[slot], slope)
        grad_k = dot(slope, q_ref[j, :, 0:DH])
        grad_v = dot(attend, grad[j])

        def finish():
            acc_q[j] += grad_q
            acc_k[slot] += grad_k
            acc_v[slot] += grad_v

        return finish

    sweep(meta_ref, list_ref, one, 0)
    for rel, out in enumerate((own_ref, s1_ref, s2_ref, s3_ref)):
        for half in (0, 1):
            rows = slice(half * HALF, (half + 1) * HALF)
            out[rows, 0:DH] = (acc_k[rel * 2 + half] * 2.0).astype(out.dtype)
            out[rows, DH : 2 * DH] = (acc_v[rel * 2 + half] * 2.0).astype(out.dtype)
    for rel in (0, 1):
        for half in (0, 1):
            rows = slice(rel * ROWS + half * HALF, rel * ROWS + (half + 1) * HALF)
            keep_ref[rows, :] = acc_q[half * GROUP + rel].T * FACTOR
            send_ref[rows, :] = (acc_q[half * GROUP + rel + 2].T * FACTOR).astype(BF)


def tail_kernel(
    meta_ref, own, r1, r2, r3, keep, got_core, got_z, grad_gate, slope, w, xa, wout_terms,
    t0_ref, t1_ref, t2_ref, t3_ref, stay_ref, away_ref,
    grad, full,
):
    core, y = meta_ref[3], meta_ref[5]
    kv = own[...] + r1[...].astype(F32) + r2[...].astype(F32) + r3[...].astype(F32)
    query = keep[0:ROWS, :] + got_core[0:ROWS, :].astype(F32) + got_z[...].astype(F32)
    grad[:, 0:DH] = grad_gate[...]
    grad[:, DH : 2 * DH] = (kv[:, DH:] * slope[:, DH : 2 * DH]).astype(BF)
    grad[:, 2 * DH : 3 * DH] = (query * slope[:, 2 * DH : 3 * DH]).astype(BF)
    grad[:, 3 * DH :] = (kv[:, 0:DH] * slope[:, 3 * DH :]).astype(BF)
    for rel, out in enumerate((t0_ref, t1_ref, t2_ref, t3_ref)):
        rows = w[pl.ds(pl.multiple_of((y ^ rel) * DH, DH), DH), :]
        out[...] = dot(grad[...], rows, NT).astype(out.dtype)
    full[0:WIDTH, :] = dot(xa[0:ROWS, :], grad[...], TN)
    full[WIDTH:, :] = wout_terms[...]
    size = full.shape[0] // 2
    stay_ref[...] = full[pl.ds(pl.multiple_of(core * size, 64), size), :]
    away_ref[...] = full[pl.ds(pl.multiple_of((1 - core) * size, 64), size), :].astype(BF)


def gather_kernel(p0, p1, p2, p3, t0, t1, t2, t3, total_ref, grad_ref):
    total = p0[...] + p1[...].astype(F32) + p2[...].astype(F32) + p3[...].astype(F32)
    total_ref[...] = total.astype(BF)
    grad = t0[...] + t1[...].astype(F32) + t2[...].astype(F32) + t3[...].astype(F32)
    grad_ref[...] = grad.astype(BF)


def add_kernel(a_ref, b_ref, _, out_ref):
    out_ref[...] = (a_ref[...].astype(F32) + b_ref[...].astype(F32)).astype(BF)


def split_kernel(meta_ref, stay, got, p0_ref, p1_ref, p2_ref, p3_ref, total):
    x = meta_ref[2]
    total[...] = stay[...] + got[...].astype(F32)
    for rel, out in enumerate((p0_ref, p1_ref, p2_ref, p3_ref)):
        rows = pl.ds(pl.multiple_of((x ^ rel) * PIECE, 16), PIECE)
        out[...] = total[rows, :].astype(out.dtype)


def join_kernel(meta_ref, p0, p1, p2, p3, out_ref):
    x = meta_ref[2]
    for rel, piece in enumerate((p0, p1, p2, p3)):
        out_ref[pl.ds(pl.multiple_of((x ^ rel) * PIECE, 16), PIECE), :] = piece[...]


def final_kernel(scale, meta_ref, mine, other, win_ref, wout_ref, full):
    core = meta_ref[3]
    size = full.shape[0] // 2
    full[pl.ds(pl.multiple_of(core * size, 64), size), :] = mine[...].astype(F32) * scale
    full[pl.ds(pl.multiple_of((1 - core) * size, 64), size), :] = other[...].astype(F32) * scale
    win_ref[...] = full[0:WIDTH, :]
    wout_ref[...] = full[WIDTH:, :]


def body(layer_input, grad_output, weight_in, weight_out, time_table, user_lengths, time_buckets):
    lengths = jnp.pad(user_lengths, ((0, 0), (0, DH - 3)))
    (xa,) = call(
        prepare_kernel,
        [((ROWS + 16, WIDTH), BF)],
        (layer_input[0], time_buckets, lengths),
    )
    xa = lax.ppermute(xa, TRANSPOSED, SWAP)

    core = lax.axis_index("core")
    x = 2 * lax.axis_index("xh") + lax.axis_index("xl")
    z = lax.axis_index("z0")
    lengths = PAD_ROWS * xa[ROWS + 1, 0:2].astype(jnp.int32)
    places = jnp.stack([x, core, z, lax.axis_index("y"), 0 * x, 0 * x])
    meta = jnp.concatenate(
        [lengths[0:1], lengths[0:1] + lengths[1:2], places.astype(jnp.int32)]
    )

    (grad_gated,) = call(
        gated_kernel, [((ROWS, DH), BF)], (grad_output[0], weight_out)
    )
    kv, q, gate, slope, grad_gated = call(
        project_kernel,
        [((ROWS + 16, 2 * DH), BF), ((ROWS, 2 * DH), BF), ((ROWS, DH), BF), ((ROWS, WIDTH), F32)],
        (xa, weight_in, time_table, grad_gated),
        passed=1,
        flops=2 * ROWS * WIDTH * WIDTH,
    )
    kvs = [kv] + [lax.ppermute(kv, ("xh", "xl"), flip_x(rel)) for rel in (1, 3, 2)]
    kvs = [kvs[0], kvs[1], kvs[3], kvs[2]]
    grad_gated = lax.ppermute(grad_gated, TRANSPOSED, SWAP)
    q_z = lax.ppermute(q, "z0", FLIP)
    qs = [q, q_z, lax.ppermute(q, "core", FLIP), lax.ppermute(q_z, "core", FLIP)]

    blocks = 2 * GROUP
    keep, send, k_all, v_all, q_all, pairs = call(
        forward_kernel,
        [
            ((2 * ROWS, DH), F32),
            ((2 * ROWS, DH), BF),
            ((blocks, HALF, 2 * DH), BF),
            ((blocks, HALF, DH), BF),
            ((blocks, HALF, 2 * DH), BF),
            ((LIST,), jnp.int32),
        ],
        (meta, *kvs, *qs, grad_gated),
        unread=1,
        scratch=[pltpu.VMEM((blocks, HALF, DH), F32)],
        flops=20 * 6 * HALF * HALF * DH,
    )
    got_core = lax.ppermute(send, "core", FLIP)
    part = (keep[ROWS:] + got_core[ROWS:].astype(F32)).astype(BF)
    got_z = lax.ppermute(part, "z0", FLIP)

    grad, grad_gate, gated = call(
        middle_kernel,
        [((ROWS, DH), BF)] * 3,
        (meta, keep, got_core, got_z, grad_gated, gate, slope),
        flops=2 * ROWS * WIDTH * DH,
    )
    grad_z = lax.ppermute(grad, "z0", FLIP)
    grads = [grad, grad_z, lax.ppermute(grad, "core", FLIP), lax.ppermute(grad_z, "core", FLIP)]
    gated = lax.ppermute(gated, TRANSPOSED, SWAP)
    wout_terms = dot(gated, grad_output[0], TN)

    own, s1, s2, s3, keep, send = call(
        backward_kernel,
        [((ROWS, 2 * DH), F32)]
        + [((ROWS, 2 * DH), BF)] * 3
        + [((2 * ROWS, DH), F32), ((2 * ROWS, DH), BF)],
        (meta, pairs, k_all, v_all, q_all, *grads),
        scratch=[
            pltpu.VMEM((blocks, HALF, DH), BF),
            pltpu.VMEM((blocks, DH, HALF), BF),
            pltpu.VMEM((blocks, HALF, DH), F32),
            pltpu.VMEM((blocks, HALF, DH), F32),
            pltpu.VMEM((blocks, DH, HALF), F32),
        ],
        flops=20 * 12 * HALF * HALF * DH,
    )
    r1 = lax.ppermute(s1, ("xh", "xl"), flip_x(1))
    r3 = lax.ppermute(s3, ("xh", "xl"), flip_x(3))
    r2 = lax.ppermute(s2, ("xh", "xl"), flip_x(2))
    got_core = lax.ppermute(send, "core", FLIP)
    part = (keep[ROWS:] + got_core[ROWS:].astype(F32)).astype(BF)
    got_z = lax.ppermute(part, "z0", FLIP)

    t0, t1, t2, t3, stay, away = call(
        tail_kernel,
        [((ROWS, DH), F32)] + [((ROWS, DH), BF)] * 3 + [((320, WIDTH), F32), ((320, WIDTH), BF)],
        (meta, own, r1, r2, r3, keep, got_core, got_z, grad_gate, slope, weight_in, xa, wout_terms),
        scratch=[pltpu.VMEM((ROWS, WIDTH), BF), pltpu.VMEM((WIDTH + DH, WIDTH), F32)],
        flops=4 * ROWS * WIDTH * WIDTH,
    )
    got = lax.ppermute(away, "core", FLIP)
    flip_y = [[(i, i ^ rel) for i in range(4)] for rel in range(4)]
    u1, u3, u2 = (lax.ppermute(t, "y", flip_y[rel]) for t, rel in ((t1, 1), (t3, 3), (t2, 2)))

    p0, p1, p2, p3 = call(
        split_kernel,
        [((PIECE, WIDTH), F32)] + [((PIECE, WIDTH), BF)] * 3,
        (meta, stay, got),
        scratch=[pltpu.VMEM((GROUP * PIECE, WIDTH), F32)],
    )
    g1, g3, g2 = (
        lax.ppermute(p, ("xh", "xl"), flip_x(rel)) for p, rel in ((p1, 1), (p3, 3), (p2, 2))
    )
    total, grad_local = call(
        gather_kernel,
        [((PIECE, WIDTH), BF), ((ROWS, DH), BF)],
        (p0, g1, g2, g3, t0, u1, u2, u3),
    )
    grad_local = lax.ppermute(grad_local, TRANSPOSED, SWAP)
    other = lax.ppermute(total, "z0", FLIP)
    total = (total.astype(F32) + other.astype(F32)).astype(BF)
    other = lax.ppermute(total, "z1", FLIP)
    total = (total.astype(F32) + other.astype(F32)).astype(BF)
    other = lax.ppermute(total, "z2", FLIP)
    (total,) = call(add_kernel, [((PIECE, WIDTH), BF)], (total, other, grad_local), unread=1)
    h1, h3, h2 = (lax.ppermute(total, ("xh", "xl"), flip_x(rel)) for rel in (1, 3, 2))
    (mine_half,) = call(join_kernel, [((320, WIDTH), BF)], (meta, total, h1, h2, h3))
    other_half = lax.ppermute(mine_half, "core", FLIP)
    normalizer = 1.0 / math.sqrt(4 * 16 * ROWS)
    win, wout = call(
        functools.partial(final_kernel, normalizer),
        [((WIDTH, WIDTH), F32), ((DH, WIDTH), F32)],
        (meta, mine_half, other_half),
        scratch=[pltpu.VMEM((WIDTH + DH, WIDTH), F32)],
    )
    return (grad_local[None], win, wout)


def solution(mesh):
    names = ("xh", "z2", "z1", "z0", "xl", "core", "y")
    fine = Mesh(mesh.devices.reshape(2, 2, 2, 2, 2, 2, 4), names)
    dp, seq = ("xl", "core"), ("xh", "z2", "z1", "z0")
    placed = (
        P(dp, seq, None),
        P(dp, seq, None),
        P(None, "y"),
        P("y", None),
        P("y", None),
        P(dp, None),
        P(dp, seq),
    )
    return jax.shard_map(
        body,
        mesh=fine,
        in_specs=placed,
        out_specs=(P(dp, seq, "y"), P(None, "y"), P("y", None)),
        check_vma=False,
    )
```

```python
import functools
import math

import jax
import jax.numpy as jnp
from jax import lax
from jax.experimental import pallas as pl
from jax.experimental.pallas import tpu as pltpu
from jax.sharding import Mesh
from jax.sharding import PartitionSpec as P

PAD_ROWS = 128
EPSILON = 0.05
ROWS = 512
HALF = 256
DH = 128
NB = 128
WIDTH = 512
GROUP = 4
BIG = 1 << 24
BF = jnp.bfloat16
F32 = jnp.float32
FACTOR = 1.0 / math.sqrt(DH)
PIECE = 80
LIST = 128

MOVED = ("z2", "z1", "z0", "xl", "core")
AWAY = [
    (16 * a + 8 * b + 4 * c + 2 * d + e, 16 * e + 8 * d + 4 * c + 2 * (b ^ c) + (a ^ b))
    for a in (0, 1)
    for b in (0, 1)
    for c in (0, 1)
    for d in (0, 1)
    for e in (0, 1)
]
HOME = [(b, a) for a, b in AWAY]
FLIP = [(0, 1), (1, 0)]


def flip_x(rel):
    return [(i, i ^ rel) for i in range(4)]


def row_index(x, core, z):
    middle = (x % 2) ^ z
    return 8 * (x // 2) + 4 * (core ^ middle) + 2 * middle + z


def dot(a, b, dims=((1,), (0,))):
    return lax.dot_general(a, b, (dims, ((), ())), preferred_element_type=F32)


NT = ((1,), (1,))
TN = ((0,), (0,))


def call(kernel, outs, args, scratch=(), flops=0, unread=0, passed=0, held=0, limit=40):
    specs = [pl.BlockSpec(memory_space=pltpu.VMEM)] * (len(args) - unread - passed)
    specs += [pl.BlockSpec(memory_space=pl.ANY)] * (unread + passed)
    specs[:held] = [pl.BlockSpec(memory_space=pltpu.HBM)] * held
    for n, a in enumerate(args):
        if a.ndim == 1:
            specs[n] = pl.BlockSpec(memory_space=pltpu.SMEM)
    before = len(outs)
    outs = list(outs) + [(a.shape, a.dtype) for a in args[len(args) - passed :]]
    out_specs = [pl.BlockSpec(memory_space=pltpu.VMEM)] * before
    out_specs += [pl.BlockSpec(memory_space=pl.ANY)] * passed
    for n, (shape, _) in enumerate(outs):
        if len(shape) == 1:
            out_specs[n] = pl.BlockSpec(memory_space=pltpu.SMEM)
    moved = sum(a.size * a.dtype.itemsize for a in args)
    moved += sum(math.prod(s) * jnp.dtype(t).itemsize for s, t in outs)
    return pl.pallas_call(
        kernel,
        out_shape=[jax.ShapeDtypeStruct(s, t) for s, t in outs],
        in_specs=specs,
        out_specs=out_specs,
        input_output_aliases={len(args) - passed + n: before + n for n in range(passed)},
        scratch_shapes=list(scratch),
        compiler_params=pltpu.CompilerParams(vmem_limit_bytes=limit * 1024 * 1024),
        cost_estimate=pl.CostEstimate(flops=flops, bytes_accessed=moved, transcendentals=0),
    )(*args)


def prepare_kernel(
    x_hbm, times_hbm, lengths_hbm, upstream_hbm, out_ref, times_ref, lengths_ref, sems
):
    quarter = pl.ds(pl.multiple_of(lax.axis_index("y") * DH, DH), DH)
    pairs = (
        (times_hbm, times_ref),
        (lengths_hbm, lengths_ref),
        (x_hbm.at[quarter, :], out_ref.at[0:DH, :]),
        (upstream_hbm.at[quarter, :], out_ref.at[DH + 16 :, :]),
    )
    copies = [pltpu.make_async_copy(a, b, sems.at[n]) for n, (a, b) in enumerate(pairs)]
    for copy in copies:
        copy.start()
    for copy in copies[:2]:
        copy.wait()
    row = lax.broadcasted_iota(jnp.int32, (16, WIDTH), 0)
    column = lax.broadcasted_iota(jnp.int32, (16, WIDTH), 1)
    lengths = lengths_ref[...].astype(F32)
    lengths = jnp.where(column == 0, lengths[:, 0:1], lengths[:, 1:2])
    times = times_ref[...].astype(F32)
    extra = jnp.where(row == 0, times, jnp.where(row == 1, lengths, 0.0))
    out_ref[DH : DH + 16, :] = extra.astype(BF)
    for copy in copies[2:]:
        copy.wait()


def project_kernel(
    _, xa_ref, x1, x2, x3, w_ref, table_ref, kv_ref, q_ref, gate_ref, slope_ref, x_ref
):
    y = lax.axis_index("y")
    for rel, piece in enumerate((xa_ref, x1, x2, x3)):
        x_ref[pl.ds(pl.multiple_of((y ^ rel) * DH, DH), DH), :] = piece[0:DH, :]
    projected = dot(x_ref[...], w_ref[...])
    sig = 0.5 + 0.5 * jnp.tanh(0.5 * projected)
    act = projected * sig
    slope_ref[...] = sig * (1.0 + projected * (1.0 - sig))
    gate_ref[...] = act[:, 0:DH].astype(BF)
    kv_ref[0:ROWS, DH : 2 * DH] = act[:, DH : 2 * DH].astype(BF)
    q_ref[:, 0:DH] = (act[:, 2 * DH : 3 * DH] * (0.5 * FACTOR)).astype(BF)
    kv_ref[0:ROWS, 0:DH] = act[:, 3 * DH : 4 * DH].astype(BF)
    times = xa_ref[DH : DH + 16, :].astype(F32)[0:1, :]
    row = lax.broadcasted_iota(jnp.int32, (16, HALF), 0)
    extra = jnp.where(row == 0, times[:, 0:HALF], jnp.where(row == 1, times[:, HALF:], 0.0))
    kv_ref[ROWS : ROWS + 16, :] = extra.astype(BF)
    table = jnp.broadcast_to(table_ref[...] * 0.5, (NB, NB))
    rolled = pltpu.roll(table, 0, 1, stride=1, stride_axis=0)
    first = lax.broadcasted_iota(jnp.int32, (NB, NB), 0)
    second = lax.broadcasted_iota(jnp.int32, (NB, NB), 1)
    square = jnp.where(second >= first, rolled, rolled.T).astype(BF)
    bucket = lax.broadcasted_iota(jnp.int32, (NB, ROWS), 0).astype(F32)
    hot = (bucket == times).astype(F32).astype(BF)
    q_ref[:, DH : 2 * DH] = dot(square, hot).T.astype(BF)


def first_of(rows, first_end, second_end):
    return jnp.where(rows < first_end, 0, jnp.where(rows < second_end, first_end, BIG))


def key_row_of(meta_ref, slot):
    x, core, z = (meta_ref[n] for n in range(2, 5))
    owner = x ^ (slot // 2)
    index = row_index(owner, core, z)
    return jnp.where(slot % 2 == 0, index, 31 - index) * HALF


def query_row_of(meta_ref, j):
    x, core, z = (meta_ref[n] for n in range(2, 5))
    rel = j % GROUP
    index = row_index(x, core ^ (rel // 2), z ^ (rel % 2))
    return jnp.where(j < GROUP, index, 31 - index) * HALF


def list_kernel(meta_ref, list_ref):
    first_end, second_end = meta_ref[0], meta_ref[1]

    def queries(j, count):
        row = query_row_of(meta_ref, j)
        lowest = first_of(row, first_end, second_end)

        def keys(slot, count):
            key_row = key_row_of(meta_ref, slot)
            valid = (key_row <= row) & (key_row + HALF > lowest)
            list_ref[count] = j * 8 + slot
            return count + valid.astype(jnp.int32)

        return lax.fori_loop(0, 2 * GROUP, keys, count, unroll=True)

    count = lax.fori_loop(0, 2 * GROUP, queries, jnp.int32(0))
    list_ref[LIST - 1] = count


def sweep(meta_ref, list_ref, one, key_axis, size):
    def several(first, number):
        done = []
        for n in range(number):
            item = list_ref[first + n]
            j, slot = item // 8, item % 8
            rows, key_rows = query_row_of(meta_ref, j), key_row_of(meta_ref, slot)
            mask = mask_of(rows, key_rows, meta_ref[0], meta_ref[1], key_axis)
            done.append(one(j, slot, mask))
        for finish in done:
            finish()

    def step(i, carry):
        several(i * size, size)
        return carry

    def rest(i, carry):
        several(i, 1)
        return carry

    count = list_ref[LIST - 1]
    lax.fori_loop(0, count // size, step, 0)
    lax.fori_loop(count // size * size, count, rest, 0)


def mask_of(query_row, key_row, first_end, second_end, key_axis):
    shape_q = (HALF, 1) if key_axis == 1 else (1, HALF)
    rows_q = query_row + lax.broadcasted_iota(jnp.int32, shape_q, 1 - key_axis)
    rows_k = key_row + lax.broadcasted_iota(jnp.int32, (HALF, HALF), key_axis)
    return (rows_k <= rows_q) & (rows_k >= first_of(rows_q, first_end, second_end))


def forward_kernel(
    meta_ref, kv0, kv1, kv2, kv3, q0, q1, q2, q3, list_ref,
    keep_ref, send_ref, k_ref, v_ref, q_ref, acc,
):
    bucket = lax.broadcasted_iota(jnp.int32, (NB, HALF), 0).astype(F32)
    for rel, kv in enumerate((kv0, kv1, kv2, kv3)):
        tail = kv[ROWS : ROWS + 16, :].astype(F32)
        for half in (0, 1):
            rows = slice(half * HALF, (half + 1) * HALF)
            hot = (bucket == tail[half : half + 1, :]).astype(F32)
            k_ref[rel * 2 + half, :, 0:DH] = kv[rows, 0:DH]
            k_ref[rel * 2 + half, :, DH : 2 * DH] = hot.T.astype(BF)
            v_ref[rel * 2 + half] = kv[rows, DH : 2 * DH]
    for rel, q in enumerate((q0, q1, q2, q3)):
        for half in (0, 1):
            q_ref[half * GROUP + rel] = q[half * HALF : (half + 1) * HALF, :]
    acc[...] = jnp.zeros_like(acc)

    def one(j, slot, mask):
        scores = dot(q_ref[j], k_ref[slot], NT)
        attend = jnp.where(mask, scores + scores * jnp.tanh(scores), 0.0)
        result = dot(attend.astype(BF), v_ref[slot])

        def finish():
            acc[j] += result

        return finish

    sweep(meta_ref, list_ref, one, 1, 4)
    for rel in (0, 1):
        for half in (0, 1):
            rows = slice(rel * ROWS + half * HALF, rel * ROWS + (half + 1) * HALF)
            keep_ref[rows, :] = acc[half * GROUP + rel]
            send_ref[rows, :] = acc[half * GROUP + rel + 2].astype(BF)


def middle_kernel(
    meta_ref, keep, got_core, got_z, up0, up1, up2, up3, wout, gate, slope,
    grad_ref, gate_ref, gated_ref,
    grad_gated_ref, gated,
):
    y = meta_ref[5]
    for rel, up in enumerate((up0, up1, up2, up3)):
        rows = pl.ds(pl.multiple_of((y ^ rel) * DH, DH), DH)
        grad_gated_ref[rows, :] = dot(up[DH + 16 :, :], wout[...], NT)
    first_end, second_end, x, core, z = (meta_ref[n] for n in range(5))
    block = row_index(x, core, z)
    offset = lax.broadcasted_iota(jnp.int32, (ROWS, 1), 0)
    rows = jnp.where(offset < HALF, block * HALF + offset, (31 - block) * HALF + offset - HALF)
    first = jnp.where(rows < first_end, 0, jnp.where(rows < second_end, first_end, second_end))
    inverse = 1.0 / jnp.maximum(rows - first + 1, 1).astype(F32)
    total = keep[0:ROWS, :] + got_core[0:ROWS, :].astype(F32) + got_z[...].astype(F32)
    attended = total * inverse
    spread = 1.0 / jnp.sqrt(jnp.mean(attended * attended, axis=-1, keepdims=True) + EPSILON)
    normed = attended * spread
    gate_float = gate[...].astype(F32)
    gated[...] = (normed * gate_float).astype(BF)
    for rel in range(GROUP):
        rows = pl.ds(pl.multiple_of((y ^ rel) * DH, DH), DH)
        gated_ref[rel * DH : (rel + 1) * DH, :] = gated[rows, :]
    grad_gated = grad_gated_ref[...]
    gate_ref[...] = (grad_gated * normed * slope[:, 0:DH]).astype(BF)
    grad_normed = grad_gated * gate_float
    inner = jnp.mean(grad_normed * normed, axis=-1, keepdims=True)
    grad_ref[...] = ((grad_normed - normed * inner) * (spread * inverse * 0.5)).astype(BF)


def backward_kernel(
    meta_ref, list_ref, k_ref, v_ref, q_ref, g0, g1, g2, g3,
    own_ref, s1_ref, s2_ref, s3_ref, keep_ref, send_ref,
    grad, kt, acc_k, acc_v, acc_q,
):
    for rel, g in enumerate((g0, g1, g2, g3)):
        for half in (0, 1):
            grad[half * GROUP + rel] = g[half * HALF : (half + 1) * HALF, :]
    for slot in range(2 * GROUP):
        kt[slot] = k_ref[slot, :, 0:DH].astype(F32).T.astype(BF)
    acc_k[...] = jnp.zeros_like(acc_k)
    acc_v[...] = jnp.zeros_like(acc_v)
    acc_q[...] = jnp.zeros_like(acc_q)

    def one(j, slot, mask):
        scores = dot(k_ref[slot], q_ref[j], NT)
        raw = dot(v_ref[slot], grad[j], NT)
        tanh = jnp.tanh(scores)
        more = 1.0 + tanh
        attend = scores * more
        slope = jnp.where(mask, raw * (more + attend * (1.0 - tanh)), 0.0).astype(BF)
        attend = jnp.where(mask, attend, 0.0).astype(BF)
        grad_q = dot(kt[slot], slope)
        grad_k = dot(slope, q_ref[j, :, 0:DH])
        grad_v = dot(attend, grad[j])

        def finish():
            acc_q[j] += grad_q
            acc_k[slot] += grad_k
            acc_v[slot] += grad_v

        return finish

    sweep(meta_ref, list_ref, one, 0, 4)
    for rel, out in enumerate((own_ref, s1_ref, s2_ref, s3_ref)):
        for half in (0, 1):
            rows = slice(half * HALF, (half + 1) * HALF)
            out[rows, 0:DH] = (acc_k[rel * 2 + half] * 2.0).astype(out.dtype)
            out[rows, DH : 2 * DH] = (acc_v[rel * 2 + half] * 2.0).astype(out.dtype)
    for rel in (0, 1):
        for half in (0, 1):
            rows = slice(rel * ROWS + half * HALF, rel * ROWS + (half + 1) * HALF)
            keep_ref[rows, :] = acc_q[half * GROUP + rel].T * FACTOR
            send_ref[rows, :] = (acc_q[half * GROUP + rel + 2].T * FACTOR).astype(BF)


def wout_kernel(gated, up0, up1, up2, up3, out_ref):
    total = dot(gated[0:DH, :], up0[DH + 16 :, :], TN)
    for rel, up in ((1, up1), (2, up2), (3, up3)):
        total = total + dot(gated[rel * DH : (rel + 1) * DH, :], up[DH + 16 :, :], TN)
    out_ref[...] = total


def tail_kernel(
    meta_ref, own, r1, r2, r3, keep, got_core, got_z, grad_gate, slope, w, x_all, wout_terms,
    t0_ref, t1_ref, t2_ref, t3_ref, stay_ref, away_ref,
    grad, full,
):
    core, y = meta_ref[3], meta_ref[5]
    kv = own[...] + r1[...].astype(F32) + r2[...].astype(F32) + r3[...].astype(F32)
    query = keep[0:ROWS, :] + got_core[0:ROWS, :].astype(F32) + got_z[...].astype(F32)
    grad[:, 0:DH] = grad_gate[...]
    grad[:, DH : 2 * DH] = (kv[:, DH:] * slope[:, DH : 2 * DH]).astype(BF)
    grad[:, 2 * DH : 3 * DH] = (query * slope[:, 2 * DH : 3 * DH]).astype(BF)
    grad[:, 3 * DH :] = (kv[:, 0:DH] * slope[:, 3 * DH :]).astype(BF)
    for rel, out in enumerate((t0_ref, t1_ref, t2_ref, t3_ref)):
        rows = w[pl.ds(pl.multiple_of((y ^ rel) * DH, DH), DH), :]
        out[...] = dot(grad[...], rows, NT).astype(out.dtype)
    full[0:WIDTH, :] = dot(x_all[...], grad[...], TN)
    full[WIDTH:, :] = wout_terms[...]
    size = full.shape[0] // 2
    stay_ref[...] = full[pl.ds(pl.multiple_of(core * size, 64), size), :]
    away_ref[...] = full[pl.ds(pl.multiple_of((1 - core) * size, 64), size), :].astype(BF)


def sum_kernel(p0, p1, p2, p3, _, __, ___, total_ref, *passed):
    total = p0[...] + p1[...].astype(F32) + p2[...].astype(F32) + p3[...].astype(F32)
    total_ref[...] = total.astype(BF)


def both_kernel(a, b, t0, t1, t2, t3, total_ref, grad_ref):
    total_ref[...] = (a[...].astype(F32) + b[...].astype(F32)).astype(BF)
    grad = t0[...] + t1[...].astype(F32) + t2[...].astype(F32) + t3[...].astype(F32)
    grad_ref[...] = grad.astype(BF)


def split_kernel(meta_ref, stay, got, p0_ref, p1_ref, p2_ref, p3_ref, total):
    x = meta_ref[2]
    total[...] = stay[...] + got[...].astype(F32)
    for rel, out in enumerate((p0_ref, p1_ref, p2_ref, p3_ref)):
        rows = pl.ds(pl.multiple_of((x ^ rel) * PIECE, 16), PIECE)
        out[...] = total[rows, :].astype(out.dtype)


def join_kernel(meta_ref, p0, p1, p2, p3, _, out_ref):
    x = meta_ref[2]
    for rel, piece in enumerate((p0, p1, p2, p3)):
        out_ref[pl.ds(pl.multiple_of((x ^ rel) * PIECE, 16), PIECE), :] = piece[...]


def final_kernel(scale, meta_ref, mine, other, grad, win_ref, wout_ref, grad_ref):
    swapped = meta_ref[3] == 1
    size = mine.shape[0]
    low = jnp.where(swapped, other[...].astype(F32), mine[...].astype(F32)) * scale
    high = jnp.where(swapped, mine[...].astype(F32), other[...].astype(F32)) * scale
    win_ref[0:size, :] = low
    win_ref[size:, :] = high[0 : WIDTH - size, :]
    wout_ref[...] = high[WIDTH - size :, :]
    grad_ref[0] = grad[...]


def body(layer_input, grad_output, weight_in, weight_out, time_table, user_lengths, time_buckets):
    (xa,) = call(
        prepare_kernel,
        [((2 * DH + 16, WIDTH), BF)],
        (layer_input[0], time_buckets, user_lengths, grad_output[0]),
        held=4,
        limit=60,
        scratch=[
            pltpu.VMEM((1, ROWS), jnp.int32),
            pltpu.VMEM((1, 3), jnp.int32),
            pltpu.SemaphoreType.DMA((4,)),
        ],
    )
    xa = lax.ppermute(xa, MOVED, AWAY)

    flip_y = [[(i, i ^ rel) for i in range(4)] for rel in range(4)]
    x1, x3, x2 = (lax.ppermute(xa, "y", flip_y[rel]) for rel in (1, 3, 2))
    core = lax.axis_index("core")
    x = 2 * lax.axis_index("xh") + lax.axis_index("xl")
    z = lax.axis_index("z0")
    lengths = PAD_ROWS * xa[DH + 1, 0:2].astype(jnp.int32)
    places = jnp.stack([x, core, z, lax.axis_index("y"), 0 * x, 0 * x])
    meta = jnp.concatenate(
        [lengths[0:1], lengths[0:1] + lengths[1:2], places.astype(jnp.int32)]
    )

    (pairs,) = call(list_kernel, [((LIST,), jnp.int32)], (meta,))
    kv, q, gate, slope, x_all = call(
        project_kernel,
        [((ROWS + 16, 2 * DH), BF), ((ROWS, 2 * DH), BF), ((ROWS, DH), BF), ((ROWS, WIDTH), F32)]
        + [((ROWS, WIDTH), BF)],
        (pairs, xa, x1, x2, x3, weight_in, time_table),
        flops=2 * ROWS * WIDTH * WIDTH,
    )
    kvs = [kv] + [lax.ppermute(kv, ("xh", "xl"), flip_x(rel)) for rel in (1, 3, 2)]
    kvs = [kvs[0], kvs[1], kvs[3], kvs[2]]
    q_z = lax.ppermute(q, "z0", FLIP)
    qs = [q, q_z, lax.ppermute(q, "core", FLIP), lax.ppermute(q_z, "core", FLIP)]

    blocks = 2 * GROUP
    keep, send, k_all, v_all, q_all = call(
        forward_kernel,
        [
            ((2 * ROWS, DH), F32),
            ((2 * ROWS, DH), BF),
            ((blocks, HALF, 2 * DH), BF),
            ((blocks, HALF, DH), BF),
            ((blocks, HALF, 2 * DH), BF),
        ],
        (meta, *kvs, *qs, pairs),
        scratch=[pltpu.VMEM((blocks, HALF, DH), F32)],
        flops=20 * 6 * HALF * HALF * DH,
    )
    got_core = lax.ppermute(send, "core", FLIP)
    part = (keep[ROWS:] + got_core[ROWS:].astype(F32)).astype(BF)
    got_z = lax.ppermute(part, "z0", FLIP)

    grad, grad_gate, gated = call(
        middle_kernel,
        [((ROWS, DH), BF)] * 3,
        (meta, keep, got_core, got_z, xa, x1, x2, x3, weight_out, gate, slope),
        scratch=[pltpu.VMEM((ROWS, DH), F32), pltpu.VMEM((ROWS, DH), BF)],
        flops=2 * ROWS * WIDTH * DH,
    )
    grad_z = lax.ppermute(grad, "z0", FLIP)
    grads = [grad, grad_z, lax.ppermute(grad, "core", FLIP), lax.ppermute(grad_z, "core", FLIP)]

    own, s1, s2, s3, keep, send = call(
        backward_kernel,
        [((ROWS, 2 * DH), F32)]
        + [((ROWS, 2 * DH), BF)] * 3
        + [((2 * ROWS, DH), F32), ((2 * ROWS, DH), BF)],
        (meta, pairs, k_all, v_all, q_all, *grads),
        scratch=[
            pltpu.VMEM((blocks, HALF, DH), BF),
            pltpu.VMEM((blocks, DH, HALF), BF),
            pltpu.VMEM((blocks, HALF, DH), F32),
            pltpu.VMEM((blocks, HALF, DH), F32),
            pltpu.VMEM((blocks, DH, HALF), F32),
        ],
        flops=20 * 12 * HALF * HALF * DH,
    )
    r1 = lax.ppermute(s1, ("xh", "xl"), flip_x(1))
    r3 = lax.ppermute(s3, ("xh", "xl"), flip_x(3))
    r2 = lax.ppermute(s2, ("xh", "xl"), flip_x(2))
    got_core = lax.ppermute(send, "core", FLIP)
    part = (keep[ROWS:] + got_core[ROWS:].astype(F32)).astype(BF)
    got_z = lax.ppermute(part, "z0", FLIP)
    (wout_terms,) = call(wout_kernel, [((DH, WIDTH), F32)], (gated, xa, x1, x2, x3))

    t0, t1, t2, t3, stay, away = call(
        tail_kernel,
        [((ROWS, DH), F32)] + [((ROWS, DH), BF)] * 3 + [((320, WIDTH), F32), ((320, WIDTH), BF)],
        (meta, own, r1, r2, r3, keep, got_core, got_z, grad_gate, slope, weight_in, x_all, wout_terms),
        scratch=[pltpu.VMEM((ROWS, WIDTH), BF), pltpu.VMEM((WIDTH + DH, WIDTH), F32)],
        flops=4 * ROWS * WIDTH * WIDTH,
    )
    got = lax.ppermute(away, "core", FLIP)
    p0, p1, p2, p3 = call(
        split_kernel,
        [((PIECE, WIDTH), F32)] + [((PIECE, WIDTH), BF)] * 3,
        (meta, stay, got),
        scratch=[pltpu.VMEM((GROUP * PIECE, WIDTH), F32)],
    )
    g1, g3, g2 = (
        lax.ppermute(p, ("xh", "xl"), flip_x(rel)) for p, rel in ((p1, 1), (p3, 3), (p2, 2))
    )
    total, t1, t2, t3 = call(
        sum_kernel, [((PIECE, WIDTH), BF)], (p0, g1, g2, g3, t1, t2, t3), passed=3
    )
    u1, u3, u2 = (lax.ppermute(t, "y", flip_y[rel]) for t, rel in ((t1, 1), (t3, 3), (t2, 2)))
    other = lax.ppermute(total, "z0", FLIP)
    total = (total.astype(F32) + other.astype(F32)).astype(BF)
    other = lax.ppermute(total, "z1", FLIP)
    total, grad_local = call(
        both_kernel,
        [((PIECE, WIDTH), BF), ((ROWS, DH), BF)],
        (total, other, t0, u1, u2, u3),
    )
    grad_local = lax.ppermute(grad_local, MOVED, HOME)
    other = lax.ppermute(total, "z2", FLIP)
    total = (total.astype(F32) + other.astype(F32)).astype(BF)
    h1, h3, h2 = (lax.ppermute(total, ("xh", "xl"), flip_x(rel)) for rel in (1, 3, 2))
    (mine_half,) = call(join_kernel, [((320, WIDTH), BF)], (meta, total, h1, h2, h3, grad_local), unread=1)
    other_half = lax.ppermute(mine_half, "core", FLIP)
    normalizer = 1.0 / math.sqrt(4 * 16 * ROWS)
    win, wout, grad_local = call(
        functools.partial(final_kernel, normalizer),
        [((WIDTH, WIDTH), F32), ((DH, WIDTH), F32), ((1, ROWS, DH), BF)],
        (meta, mine_half, other_half, grad_local),
    )
    return (grad_local, win, wout)


def solution(mesh):
    names = ("xh", "z2", "z1", "z0", "xl", "core", "y")
    fine = Mesh(mesh.devices.reshape(2, 2, 2, 2, 2, 2, 4), names)
    dp, seq = ("xl", "core"), ("xh", "z2", "z1", "z0")
    placed = (
        P(dp, seq, None),
        P(dp, seq, None),
        P(None, "y"),
        P("y", None),
        P("y", None),
        P(dp, None),
        P(dp, seq),
    )
    return jax.shard_map(
        body,
        mesh=fine,
        in_specs=placed,
        out_specs=(P(dp, seq, "y"), P(None, "y"), P("y", None)),
        check_vma=False,
    )
```

```python
import functools
import math

import jax
import jax.numpy as jnp
from jax import lax
from jax.experimental import pallas as pl
from jax.experimental.pallas import tpu as pltpu
from jax.sharding import Mesh
from jax.sharding import PartitionSpec as P

PAD_ROWS = 128
EPSILON = 0.05
ROWS = 512
HALF = 256
DH = 128
NB = 128
WIDTH = 512
GROUP = 4
BIG = 1 << 24
BF = jnp.bfloat16
F32 = jnp.float32
FACTOR = 1.0 / math.sqrt(DH)
PIECE = 80
LIST = 128

MOVED = ("z2", "z1", "z0", "xl", "core")
AWAY = [
    (16 * a + 8 * b + 4 * c + 2 * d + e, 16 * e + 8 * d + 4 * c + 2 * (b ^ c) + (a ^ b))
    for a in (0, 1)
    for b in (0, 1)
    for c in (0, 1)
    for d in (0, 1)
    for e in (0, 1)
]
HOME = [(b, a) for a, b in AWAY]
FLIP = [(0, 1), (1, 0)]


def flip_x(rel):
    return [(i, i ^ rel) for i in range(4)]


def row_index(x, core, z):
    middle = (x % 2) ^ z
    return 8 * (x // 2) + 4 * (core ^ middle) + 2 * middle + z


def dot(a, b, dims=((1,), (0,))):
    return lax.dot_general(a, b, (dims, ((), ())), preferred_element_type=F32)


NT = ((1,), (1,))
TN = ((0,), (0,))


def call(kernel, outs, args, scratch=(), flops=0, unread=0, passed=0, held=0, limit=40):
    specs = [pl.BlockSpec(memory_space=pltpu.VMEM)] * (len(args) - unread - passed)
    specs += [pl.BlockSpec(memory_space=pl.ANY)] * (unread + passed)
    specs[:held] = [pl.BlockSpec(memory_space=pltpu.HBM)] * held
    for n, a in enumerate(args):
        if a.ndim == 1:
            specs[n] = pl.BlockSpec(memory_space=pltpu.SMEM)
    before = len(outs)
    outs = list(outs) + [(a.shape, a.dtype) for a in args[len(args) - passed :]]
    out_specs = [pl.BlockSpec(memory_space=pltpu.VMEM)] * before
    out_specs += [pl.BlockSpec(memory_space=pl.ANY)] * passed
    for n, (shape, _) in enumerate(outs):
        if len(shape) == 1:
            out_specs[n] = pl.BlockSpec(memory_space=pltpu.SMEM)
    moved = sum(a.size * a.dtype.itemsize for a in args)
    moved += sum(math.prod(s) * jnp.dtype(t).itemsize for s, t in outs)
    return pl.pallas_call(
        kernel,
        out_shape=[jax.ShapeDtypeStruct(s, t) for s, t in outs],
        in_specs=specs,
        out_specs=out_specs,
        input_output_aliases={len(args) - passed + n: before + n for n in range(passed)},
        scratch_shapes=list(scratch),
        compiler_params=pltpu.CompilerParams(vmem_limit_bytes=limit * 1024 * 1024),
        cost_estimate=pl.CostEstimate(flops=flops, bytes_accessed=moved, transcendentals=0),
    )(*args)


def prepare_kernel(
    x_hbm, times_hbm, lengths_hbm, upstream_hbm, out_ref, times_ref, lengths_ref, sems
):
    quarter = pl.ds(pl.multiple_of(lax.axis_index("y") * DH, DH), DH)
    pairs = (
        (times_hbm, times_ref),
        (lengths_hbm, lengths_ref),
        (x_hbm.at[quarter, :], out_ref.at[0:DH, :]),
        (upstream_hbm.at[quarter, :], out_ref.at[DH + 16 :, :]),
    )
    copies = [pltpu.make_async_copy(a, b, sems.at[n]) for n, (a, b) in enumerate(pairs)]
    for copy in copies:
        copy.start()
    for copy in copies[:2]:
        copy.wait()
    row = lax.broadcasted_iota(jnp.int32, (16, WIDTH), 0)
    column = lax.broadcasted_iota(jnp.int32, (16, WIDTH), 1)
    lengths = lengths_ref[...].astype(F32)
    lengths = jnp.where(column == 0, lengths[:, 0:1], lengths[:, 1:2])
    times = times_ref[...].astype(F32)
    extra = jnp.where(row == 0, times, jnp.where(row == 1, lengths, 0.0))
    out_ref[DH : DH + 16, :] = extra.astype(BF)
    for copy in copies[2:]:
        copy.wait()


def project_kernel(
    _, xa_ref, x1, x3, x2, w_ref, table_ref, kv_ref, q_ref, gate_ref, slope_ref, x_ref
):
    y = lax.axis_index("y")
    for rel, piece in enumerate((xa_ref, x1, x2, x3)):
        x_ref[pl.ds(pl.multiple_of((y ^ rel) * DH, DH), DH), :] = piece[0:DH, :]
    projected = dot(x_ref[...], w_ref[...])
    sig = 0.5 + 0.5 * jnp.tanh(0.5 * projected)
    act = projected * sig
    slope_ref[...] = sig * (1.0 + projected * (1.0 - sig))
    gate_ref[...] = act[:, 0:DH].astype(BF)
    kv_ref[0:ROWS, DH : 2 * DH] = act[:, DH : 2 * DH].astype(BF)
    q_ref[:, 0:DH] = (act[:, 2 * DH : 3 * DH] * (0.5 * FACTOR)).astype(BF)
    kv_ref[0:ROWS, 0:DH] = act[:, 3 * DH : 4 * DH].astype(BF)
    times = xa_ref[DH : DH + 16, :].astype(F32)[0:1, :]
    row = lax.broadcasted_iota(jnp.int32, (16, HALF), 0)
    extra = jnp.where(row == 0, times[:, 0:HALF], jnp.where(row == 1, times[:, HALF:], 0.0))
    kv_ref[ROWS : ROWS + 16, :] = extra.astype(BF)
    table = jnp.broadcast_to(table_ref[...] * 0.5, (NB, NB))
    rolled = pltpu.roll(table, 0, 1, stride=1, stride_axis=0)
    first = lax.broadcasted_iota(jnp.int32, (NB, NB), 0)
    second = lax.broadcasted_iota(jnp.int32, (NB, NB), 1)
    square = jnp.where(second >= first, rolled, rolled.T).astype(BF)
    bucket = lax.broadcasted_iota(jnp.int32, (NB, ROWS), 0).astype(F32)
    hot = (bucket == times).astype(F32).astype(BF)
    q_ref[:, DH : 2 * DH] = dot(square, hot).T.astype(BF)


def first_of(rows, first_end, second_end):
    return jnp.where(rows < first_end, 0, jnp.where(rows < second_end, first_end, BIG))


def key_row_of(meta_ref, slot):
    x, core, z = (meta_ref[n] for n in range(2, 5))
    owner = x ^ (slot // 2)
    index = row_index(owner, core, z)
    return jnp.where(slot % 2 == 0, index, 31 - index) * HALF


def query_row_of(meta_ref, j):
    x, core, z = (meta_ref[n] for n in range(2, 5))
    rel = j % GROUP
    index = row_index(x, core ^ (rel // 2), z ^ (rel % 2))
    return jnp.where(j < GROUP, index, 31 - index) * HALF


def list_kernel(meta_ref, list_ref):
    first_end, second_end = meta_ref[0], meta_ref[1]

    def queries(j, count):
        row = query_row_of(meta_ref, j)
        lowest = first_of(row, first_end, second_end)

        def keys(slot, count):
            key_row = key_row_of(meta_ref, slot)
            valid = (key_row <= row) & (key_row + HALF > lowest)
            list_ref[count] = j * 8 + slot
            return count + valid.astype(jnp.int32)

        return lax.fori_loop(0, 2 * GROUP, keys, count, unroll=True)

    count = lax.fori_loop(0, 2 * GROUP, queries, jnp.int32(0))
    list_ref[LIST - 1] = count


def sweep(meta_ref, list_ref, one, key_axis, size):
    def several(first, number):
        done = []
        for n in range(number):
            item = list_ref[first + n]
            j, slot = item // 8, item % 8
            rows, key_rows = query_row_of(meta_ref, j), key_row_of(meta_ref, slot)
            mask = mask_of(rows, key_rows, meta_ref[0], meta_ref[1], key_axis)
            done.append(one(j, slot, mask))
        for finish in done:
            finish()

    def step(i, carry):
        several(i * size, size)
        return carry

    def rest(i, carry):
        several(i, 1)
        return carry

    count = list_ref[LIST - 1]
    lax.fori_loop(0, count // size, step, 0)
    lax.fori_loop(count // size * size, count, rest, 0)


def mask_of(query_row, key_row, first_end, second_end, key_axis):
    shape_q = (HALF, 1) if key_axis == 1 else (1, HALF)
    rows_q = query_row + lax.broadcasted_iota(jnp.int32, shape_q, 1 - key_axis)
    rows_k = key_row + lax.broadcasted_iota(jnp.int32, (HALF, HALF), key_axis)
    return (rows_k <= rows_q) & (rows_k >= first_of(rows_q, first_end, second_end))


def forward_kernel(
    meta_ref, kv0, kv1, kv3, kv2, q0, q1, q2, q3, list_ref,
    keep_ref, send_ref, k_ref, v_ref, q_ref, acc,
):
    bucket = lax.broadcasted_iota(jnp.int32, (NB, HALF), 0).astype(F32)
    for rel, kv in enumerate((kv0, kv1, kv2, kv3)):
        tail = kv[ROWS : ROWS + 16, :].astype(F32)
        for half in (0, 1):
            rows = slice(half * HALF, (half + 1) * HALF)
            hot = (bucket == tail[half : half + 1, :]).astype(F32)
            k_ref[rel * 2 + half, :, 0:DH] = kv[rows, 0:DH]
            k_ref[rel * 2 + half, :, DH : 2 * DH] = hot.T.astype(BF)
            v_ref[rel * 2 + half] = kv[rows, DH : 2 * DH]
    for rel, q in enumerate((q0, q1, q2, q3)):
        for half in (0, 1):
            q_ref[half * GROUP + rel] = q[half * HALF : (half + 1) * HALF, :]
    acc[...] = jnp.zeros_like(acc)

    def one(j, slot, mask):
        scores = dot(q_ref[j], k_ref[slot], NT)
        attend = jnp.where(mask, scores + scores * jnp.tanh(scores), 0.0)
        result = dot(attend.astype(BF), v_ref[slot])

        def finish():
            acc[j] += result

        return finish

    sweep(meta_ref, list_ref, one, 1, 4)
    for rel in (0, 1):
        for half in (0, 1):
            rows = slice(rel * ROWS + half * HALF, rel * ROWS + (half + 1) * HALF)
            keep_ref[rows, :] = acc[half * GROUP + rel]
            send_ref[rows, :] = acc[half * GROUP + rel + 2].astype(BF)


def middle_kernel(
    meta_ref, keep, got_core, got_z, up0, up1, up2, up3, wout, gate, slope,
    grad_ref, gate_ref, gated_ref,
    grad_gated_ref, gated,
):
    y = meta_ref[5]
    for rel, up in enumerate((up0, up1, up2, up3)):
        rows = pl.ds(pl.multiple_of((y ^ rel) * DH, DH), DH)
        grad_gated_ref[rows, :] = dot(up[DH + 16 :, :], wout[...], NT)
    first_end, second_end, x, core, z = (meta_ref[n] for n in range(5))
    block = row_index(x, core, z)
    offset = lax.broadcasted_iota(jnp.int32, (ROWS, 1), 0)
    rows = jnp.where(offset < HALF, block * HALF + offset, (31 - block) * HALF + offset - HALF)
    first = jnp.where(rows < first_end, 0, jnp.where(rows < second_end, first_end, second_end))
    inverse = 1.0 / jnp.maximum(rows - first + 1, 1).astype(F32)
    total = keep[0:ROWS, :] + got_core[0:ROWS, :].astype(F32) + got_z[...].astype(F32)
    attended = total * inverse
    spread = 1.0 / jnp.sqrt(jnp.mean(attended * attended, axis=-1, keepdims=True) + EPSILON)
    normed = attended * spread
    gate_float = gate[...].astype(F32)
    gated[...] = (normed * gate_float).astype(BF)
    for rel in range(GROUP):
        rows = pl.ds(pl.multiple_of((y ^ rel) * DH, DH), DH)
        gated_ref[rel * DH : (rel + 1) * DH, :] = gated[rows, :]
    grad_gated = grad_gated_ref[...]
    gate_ref[...] = (grad_gated * normed * slope[:, 0:DH]).astype(BF)
    grad_normed = grad_gated * gate_float
    inner = jnp.mean(grad_normed * normed, axis=-1, keepdims=True)
    grad_ref[...] = ((grad_normed - normed * inner) * (spread * inverse * 0.5)).astype(BF)


def backward_kernel(
    meta_ref, list_ref, k_ref, v_ref, q_ref, g0, g1, g2, g3,
    own_ref, s1_ref, s2_ref, s3_ref, keep_ref, send_ref,
    grad, kt, acc_k, acc_v, acc_q,
):
    for rel, g in enumerate((g0, g1, g2, g3)):
        for half in (0, 1):
            grad[half * GROUP + rel] = g[half * HALF : (half + 1) * HALF, :]
    for slot in range(2 * GROUP):
        kt[slot] = k_ref[slot, :, 0:DH].astype(F32).T.astype(BF)
    acc_k[...] = jnp.zeros_like(acc_k)
    acc_v[...] = jnp.zeros_like(acc_v)
    acc_q[...] = jnp.zeros_like(acc_q)

    def one(j, slot, mask):
        scores = dot(k_ref[slot], q_ref[j], NT)
        raw = dot(v_ref[slot], grad[j], NT)
        tanh = jnp.tanh(scores)
        more = 1.0 + tanh
        attend = scores * more
        slope = jnp.where(mask, raw * (more + attend * (1.0 - tanh)), 0.0).astype(BF)
        attend = jnp.where(mask, attend, 0.0).astype(BF)
        grad_q = dot(kt[slot], slope)
        grad_k = dot(slope, q_ref[j, :, 0:DH])
        grad_v = dot(attend, grad[j])

        def finish():
            acc_q[j] += grad_q
            acc_k[slot] += grad_k
            acc_v[slot] += grad_v

        return finish

    sweep(meta_ref, list_ref, one, 0, 4)
    for rel, out in enumerate((own_ref, s1_ref, s2_ref, s3_ref)):
        for half in (0, 1):
            rows = slice(half * HALF, (half + 1) * HALF)
            out[rows, 0:DH] = (acc_k[rel * 2 + half] * 2.0).astype(out.dtype)
            out[rows, DH : 2 * DH] = (acc_v[rel * 2 + half] * 2.0).astype(out.dtype)
    for rel in (0, 1):
        for half in (0, 1):
            rows = slice(rel * ROWS + half * HALF, rel * ROWS + (half + 1) * HALF)
            keep_ref[rows, :] = acc_q[half * GROUP + rel].T * FACTOR
            send_ref[rows, :] = (acc_q[half * GROUP + rel + 2].T * FACTOR).astype(BF)


def wout_kernel(gated, up0, up1, up2, up3, out_ref):
    total = dot(gated[0:DH, :], up0[DH + 16 :, :], TN)
    for rel, up in ((1, up1), (2, up2), (3, up3)):
        total = total + dot(gated[rel * DH : (rel + 1) * DH, :], up[DH + 16 :, :], TN)
    out_ref[...] = total


def tail_kernel(
    meta_ref, own, r2, r1, r3, keep, got_core, got_z, grad_gate, slope, w, x_all, wout_terms,
    t0_ref, t1_ref, t2_ref, t3_ref, stay_ref, away_ref,
    grad, full,
):
    core, y = meta_ref[3], meta_ref[5]
    kv = own[...] + r1[...].astype(F32) + r2[...].astype(F32) + r3[...].astype(F32)
    query = keep[0:ROWS, :] + got_core[0:ROWS, :].astype(F32) + got_z[...].astype(F32)
    grad[:, 0:DH] = grad_gate[...]
    grad[:, DH : 2 * DH] = (kv[:, DH:] * slope[:, DH : 2 * DH]).astype(BF)
    grad[:, 2 * DH : 3 * DH] = (query * slope[:, 2 * DH : 3 * DH]).astype(BF)
    grad[:, 3 * DH :] = (kv[:, 0:DH] * slope[:, 3 * DH :]).astype(BF)
    for rel, out in enumerate((t0_ref, t1_ref, t2_ref, t3_ref)):
        rows = w[pl.ds(pl.multiple_of((y ^ rel) * DH, DH), DH), :]
        out[...] = dot(grad[...], rows, NT).astype(out.dtype)
    full[0:WIDTH, :] = dot(x_all[...], grad[...], TN)
    full[WIDTH:, :] = wout_terms[...]
    size = full.shape[0] // 2
    stay_ref[...] = full[pl.ds(pl.multiple_of(core * size, 64), size), :]
    away_ref[...] = full[pl.ds(pl.multiple_of((1 - core) * size, 64), size), :].astype(BF)


def sum_kernel(p0, p1, p2, p3, _, __, ___, total_ref, *passed):
    total = p0[...] + p1[...].astype(F32) + p2[...].astype(F32) + p3[...].astype(F32)
    total_ref[...] = total.astype(BF)


def both_kernel(a, b, t0, t1, t2, t3, total_ref, grad_ref):
    total_ref[...] = (a[...].astype(F32) + b[...].astype(F32)).astype(BF)
    grad = t0[...] + t1[...].astype(F32) + t2[...].astype(F32) + t3[...].astype(F32)
    grad_ref[...] = grad.astype(BF)


def split_kernel(meta_ref, stay, got, p0_ref, p1_ref, p2_ref, p3_ref, total):
    x = meta_ref[2]
    total[...] = stay[...] + got[...].astype(F32)
    for rel, out in enumerate((p0_ref, p1_ref, p2_ref, p3_ref)):
        rows = pl.ds(pl.multiple_of((x ^ rel) * PIECE, 16), PIECE)
        out[...] = total[rows, :].astype(out.dtype)


def join_kernel(meta_ref, p0, p1, p3, p2, _, out_ref):
    x = meta_ref[2]
    for rel, piece in enumerate((p0, p1, p2, p3)):
        out_ref[pl.ds(pl.multiple_of((x ^ rel) * PIECE, 16), PIECE), :] = piece[...]


def final_kernel(scale, meta_ref, mine, other, grad, win_ref, wout_ref, grad_ref):
    swapped = meta_ref[3] == 1
    size = mine.shape[0]
    low = jnp.where(swapped, other[...].astype(F32), mine[...].astype(F32)) * scale
    high = jnp.where(swapped, mine[...].astype(F32), other[...].astype(F32)) * scale
    win_ref[0:size, :] = low
    win_ref[size:, :] = high[0 : WIDTH - size, :]
    wout_ref[...] = high[WIDTH - size :, :]
    grad_ref[0] = grad[...]


def body(layer_input, grad_output, weight_in, weight_out, time_table, user_lengths, time_buckets):
    (xa,) = call(
        prepare_kernel,
        [((2 * DH + 16, WIDTH), BF)],
        (layer_input[0], time_buckets, user_lengths, grad_output[0]),
        held=4,
        limit=60,
        scratch=[
            pltpu.VMEM((1, ROWS), jnp.int32),
            pltpu.VMEM((1, 3), jnp.int32),
            pltpu.SemaphoreType.DMA((4,)),
        ],
    )
    xa = lax.ppermute(xa, MOVED, AWAY)

    flip_y = [[(i, i ^ rel) for i in range(4)] for rel in range(4)]
    x1, x3, x2 = (lax.ppermute(xa, "y", flip_y[rel]) for rel in (1, 3, 2))
    core = lax.axis_index("core")
    x = 2 * lax.axis_index("xh") + lax.axis_index("xl")
    z = lax.axis_index("z0")
    lengths = PAD_ROWS * xa[DH + 1, 0:2].astype(jnp.int32)
    places = jnp.stack([x, core, z, lax.axis_index("y"), 0 * x, 0 * x])
    meta = jnp.concatenate(
        [lengths[0:1], lengths[0:1] + lengths[1:2], places.astype(jnp.int32)]
    )

    (pairs,) = call(list_kernel, [((LIST,), jnp.int32)], (meta,))
    kv, q, gate, slope, x_all = call(
        project_kernel,
        [((ROWS + 16, 2 * DH), BF), ((ROWS, 2 * DH), BF), ((ROWS, DH), BF), ((ROWS, WIDTH), F32)]
        + [((ROWS, WIDTH), BF)],
        (pairs, xa, x1, x3, x2, weight_in, time_table),
        flops=2 * ROWS * WIDTH * WIDTH,
    )
    kvs = [kv] + [lax.ppermute(kv, ("xh", "xl"), flip_x(rel)) for rel in (1, 3, 2)]
    kvs = [kvs[0], kvs[1], kvs[3], kvs[2]]
    q_z = lax.ppermute(q, "z0", FLIP)
    qs = [q, q_z, lax.ppermute(q, "core", FLIP), lax.ppermute(q_z, "core", FLIP)]

    blocks = 2 * GROUP
    keep, send, k_all, v_all, q_all = call(
        forward_kernel,
        [
            ((2 * ROWS, DH), F32),
            ((2 * ROWS, DH), BF),
            ((blocks, HALF, 2 * DH), BF),
            ((blocks, HALF, DH), BF),
            ((blocks, HALF, 2 * DH), BF),
        ],
        (meta, kvs[0], kvs[1], kvs[3], kvs[2], *qs, pairs),
        scratch=[pltpu.VMEM((blocks, HALF, DH), F32)],
        flops=20 * 6 * HALF * HALF * DH,
    )
    got_core = lax.ppermute(send, "core", FLIP)
    part = (keep[ROWS:] + got_core[ROWS:].astype(F32)).astype(BF)
    got_z = lax.ppermute(part, "z0", FLIP)

    grad, grad_gate, gated = call(
        middle_kernel,
        [((ROWS, DH), BF)] * 3,
        (meta, keep, got_core, got_z, xa, x1, x2, x3, weight_out, gate, slope),
        scratch=[pltpu.VMEM((ROWS, DH), F32), pltpu.VMEM((ROWS, DH), BF)],
        flops=2 * ROWS * WIDTH * DH,
    )
    grad_z = lax.ppermute(grad, "z0", FLIP)
    grads = [grad, grad_z, lax.ppermute(grad, "core", FLIP), lax.ppermute(grad_z, "core", FLIP)]

    own, s1, s2, s3, keep, send = call(
        backward_kernel,
        [((ROWS, 2 * DH), F32)]
        + [((ROWS, 2 * DH), BF)] * 3
        + [((2 * ROWS, DH), F32), ((2 * ROWS, DH), BF)],
        (meta, pairs, k_all, v_all, q_all, *grads),
        scratch=[
            pltpu.VMEM((blocks, HALF, DH), BF),
            pltpu.VMEM((blocks, DH, HALF), BF),
            pltpu.VMEM((blocks, HALF, DH), F32),
            pltpu.VMEM((blocks, HALF, DH), F32),
            pltpu.VMEM((blocks, DH, HALF), F32),
        ],
        flops=20 * 12 * HALF * HALF * DH,
    )
    r1 = lax.ppermute(s1, ("xh", "xl"), flip_x(1))
    r3 = lax.ppermute(s3, ("xh", "xl"), flip_x(3))
    r2 = lax.ppermute(s2, ("xh", "xl"), flip_x(2))
    got_core = lax.ppermute(send, "core", FLIP)
    part = (keep[ROWS:] + got_core[ROWS:].astype(F32)).astype(BF)
    got_z = lax.ppermute(part, "z0", FLIP)
    (wout_terms,) = call(wout_kernel, [((DH, WIDTH), F32)], (gated, xa, x1, x2, x3))

    t0, t1, t2, t3, stay, away = call(
        tail_kernel,
        [((ROWS, DH), F32)] + [((ROWS, DH), BF)] * 3 + [((320, WIDTH), F32), ((320, WIDTH), BF)],
        (meta, own, r2, r1, r3, keep, got_core, got_z, grad_gate, slope, weight_in, x_all, wout_terms),
        scratch=[pltpu.VMEM((ROWS, WIDTH), BF), pltpu.VMEM((WIDTH + DH, WIDTH), F32)],
        flops=4 * ROWS * WIDTH * WIDTH,
    )
    got = lax.ppermute(away, "core", FLIP)
    p0, p1, p2, p3 = call(
        split_kernel,
        [((PIECE, WIDTH), F32)] + [((PIECE, WIDTH), BF)] * 3,
        (meta, stay, got),
        scratch=[pltpu.VMEM((GROUP * PIECE, WIDTH), F32)],
    )
    g1, g3, g2 = (
        lax.ppermute(p, ("xh", "xl"), flip_x(rel)) for p, rel in ((p1, 1), (p3, 3), (p2, 2))
    )
    total, t1, t2, t3 = call(
        sum_kernel, [((PIECE, WIDTH), BF)], (p0, g2, g1, g3, t1, t2, t3), passed=3
    )
    u1, u3, u2 = (lax.ppermute(t, "y", flip_y[rel]) for t, rel in ((t1, 1), (t3, 3), (t2, 2)))
    other = lax.ppermute(total, "z2", FLIP)
    total = (total.astype(F32) + other.astype(F32)).astype(BF)
    other = lax.ppermute(total, "z1", FLIP)
    total, grad_local = call(
        both_kernel,
        [((PIECE, WIDTH), BF), ((ROWS, DH), BF)],
        (total, other, t0, u1, u2, u3),
    )
    grad_local = lax.ppermute(grad_local, MOVED, HOME)
    other = lax.ppermute(total, "z0", FLIP)
    total = (total.astype(F32) + other.astype(F32)).astype(BF)
    h1, h3, h2 = (lax.ppermute(total, ("xh", "xl"), flip_x(rel)) for rel in (1, 3, 2))
    (mine_half,) = call(join_kernel, [((320, WIDTH), BF)], (meta, total, h1, h3, h2, grad_local), unread=1)
    other_half = lax.ppermute(mine_half, "core", FLIP)
    normalizer = 1.0 / math.sqrt(4 * 16 * ROWS)
    win, wout, grad_local = call(
        functools.partial(final_kernel, normalizer),
        [((WIDTH, WIDTH), F32), ((DH, WIDTH), F32), ((1, ROWS, DH), BF)],
        (meta, mine_half, other_half, grad_local),
    )
    return (grad_local, win, wout)


def solution(mesh):
    names = ("xh", "z2", "z1", "z0", "xl", "core", "y")
    fine = Mesh(mesh.devices.reshape(2, 2, 2, 2, 2, 2, 4), names)
    dp, seq = ("xl", "core"), ("xh", "z2", "z1", "z0")
    placed = (
        P(dp, seq, None),
        P(dp, seq, None),
        P(None, "y"),
        P("y", None),
        P("y", None),
        P(dp, None),
        P(dp, seq),
    )
    return jax.shard_map(
        body,
        mesh=fine,
        in_specs=placed,
        out_specs=(P(dp, seq, "y"), P(None, "y"), P("y", None)),
        check_vma=False,
    )
```

```python
import functools
import math

import jax
import jax.numpy as jnp
from jax import lax
from jax.experimental import pallas as pl
from jax.experimental.pallas import tpu as pltpu
from jax.sharding import Mesh
from jax.sharding import PartitionSpec as P

PAD_ROWS = 128
EPSILON = 0.05
ROWS = 512
HALF = 256
DH = 128
NB = 128
WIDTH = 512
GROUP = 4
BIG = 1 << 24
BF = jnp.bfloat16
F32 = jnp.float32
FACTOR = 1.0 / math.sqrt(DH)
PIECE = 80
LIST = 128

MOVED = ("z2", "z1", "z0", "xl", "core")
AWAY = [
    (16 * a + 8 * b + 4 * c + 2 * d + e, 16 * e + 8 * d + 4 * c + 2 * (b ^ c) + (a ^ b))
    for a in (0, 1)
    for b in (0, 1)
    for c in (0, 1)
    for d in (0, 1)
    for e in (0, 1)
]
HOME = [(b, a) for a, b in AWAY]
FLIP = [(0, 1), (1, 0)]


def flip_x(rel):
    return [(i, i ^ rel) for i in range(4)]


def row_index(x, core, z):
    middle = (x % 2) ^ z
    return 8 * (x // 2) + 4 * (core ^ middle) + 2 * middle + z


def dot(a, b, dims=((1,), (0,))):
    return lax.dot_general(a, b, (dims, ((), ())), preferred_element_type=F32)


NT = ((1,), (1,))
TN = ((0,), (0,))


def call(kernel, outs, args, scratch=(), flops=0, unread=0, passed=0, held=0, limit=40):
    specs = [pl.BlockSpec(memory_space=pltpu.VMEM)] * (len(args) - unread - passed)
    specs += [pl.BlockSpec(memory_space=pl.ANY)] * (unread + passed)
    specs[:held] = [pl.BlockSpec(memory_space=pltpu.HBM)] * held
    for n, a in enumerate(args):
        if a.ndim == 1:
            specs[n] = pl.BlockSpec(memory_space=pltpu.SMEM)
    before = len(outs)
    outs = list(outs) + [(a.shape, a.dtype) for a in args[len(args) - passed :]]
    out_specs = [pl.BlockSpec(memory_space=pltpu.VMEM)] * before
    out_specs += [pl.BlockSpec(memory_space=pl.ANY)] * passed
    for n, (shape, _) in enumerate(outs):
        if len(shape) == 1:
            out_specs[n] = pl.BlockSpec(memory_space=pltpu.SMEM)
    moved = sum(a.size * a.dtype.itemsize for a in args)
    moved += sum(math.prod(s) * jnp.dtype(t).itemsize for s, t in outs)
    return pl.pallas_call(
        kernel,
        out_shape=[jax.ShapeDtypeStruct(s, t) for s, t in outs],
        in_specs=specs,
        out_specs=out_specs,
        input_output_aliases={len(args) - passed + n: before + n for n in range(passed)},
        scratch_shapes=list(scratch),
        compiler_params=pltpu.CompilerParams(vmem_limit_bytes=limit * 1024 * 1024),
        cost_estimate=pl.CostEstimate(flops=flops, bytes_accessed=moved, transcendentals=0),
    )(*args)


def prepare_kernel(
    x_hbm, times_hbm, lengths_hbm, upstream_hbm, out_ref, times_ref, lengths_ref, sems
):
    quarter = pl.ds(pl.multiple_of(lax.axis_index("y") * DH, DH), DH)
    pairs = (
        (times_hbm, times_ref),
        (lengths_hbm, lengths_ref),
        (x_hbm.at[quarter, :], out_ref.at[0:DH, :]),
        (upstream_hbm.at[quarter, :], out_ref.at[DH + 16 :, :]),
    )
    copies = [pltpu.make_async_copy(a, b, sems.at[n]) for n, (a, b) in enumerate(pairs)]
    for copy in copies:
        copy.start()
    for copy in copies[:2]:
        copy.wait()
    row = lax.broadcasted_iota(jnp.int32, (16, WIDTH), 0)
    column = lax.broadcasted_iota(jnp.int32, (16, WIDTH), 1)
    lengths = lengths_ref[...].astype(F32)
    lengths = jnp.where(column == 0, lengths[:, 0:1], lengths[:, 1:2])
    times = times_ref[...].astype(F32)
    extra = jnp.where(row == 0, times, jnp.where(row == 1, lengths, 0.0))
    out_ref[DH : DH + 16, :] = extra.astype(BF)
    for copy in copies[2:]:
        copy.wait()


def project_kernel(
    _, xa_ref, x1, x2, x3, w_ref, table_ref, kv_ref, q_ref, gate_ref, slope_ref, x_ref
):
    y = lax.axis_index("y")
    for rel, piece in enumerate((xa_ref, x1, x2, x3)):
        x_ref[pl.ds(pl.multiple_of((y ^ rel) * DH, DH), DH), :] = piece[0:DH, :]
    projected = dot(x_ref[...], w_ref[...])
    sig = 0.5 + 0.5 * jnp.tanh(0.5 * projected)
    act = projected * sig
    slope_ref[...] = sig * (1.0 + projected * (1.0 - sig))
    gate_ref[...] = act[:, 0:DH].astype(BF)
    kv_ref[0:ROWS, DH : 2 * DH] = act[:, DH : 2 * DH].astype(BF)
    q_ref[:, 0:DH] = (act[:, 2 * DH : 3 * DH] * (0.5 * FACTOR)).astype(BF)
    kv_ref[0:ROWS, 0:DH] = act[:, 3 * DH : 4 * DH].astype(BF)
    times = xa_ref[DH : DH + 16, :].astype(F32)[0:1, :]
    row = lax.broadcasted_iota(jnp.int32, (16, HALF), 0)
    extra = jnp.where(row == 0, times[:, 0:HALF], jnp.where(row == 1, times[:, HALF:], 0.0))
    kv_ref[ROWS : ROWS + 16, :] = extra.astype(BF)
    table = jnp.broadcast_to(table_ref[...] * 0.5, (NB, NB))
    rolled = pltpu.roll(table, 0, 1, stride=1, stride_axis=0)
    first = lax.broadcasted_iota(jnp.int32, (NB, NB), 0)
    second = lax.broadcasted_iota(jnp.int32, (NB, NB), 1)
    square = jnp.where(second >= first, rolled, rolled.T).astype(BF)
    bucket = lax.broadcasted_iota(jnp.int32, (NB, ROWS), 0).astype(F32)
    hot = (bucket == times).astype(F32).astype(BF)
    q_ref[:, DH : 2 * DH] = dot(square, hot).T.astype(BF)


def first_of(rows, first_end, second_end):
    return jnp.where(rows < first_end, 0, jnp.where(rows < second_end, first_end, BIG))


def key_row_of(meta_ref, slot):
    x, core, z = (meta_ref[n] for n in range(2, 5))
    owner = x ^ (slot // 2)
    index = row_index(owner, core, z)
    return jnp.where(slot % 2 == 0, index, 31 - index) * HALF


def query_row_of(meta_ref, j):
    x, core, z = (meta_ref[n] for n in range(2, 5))
    rel = j % GROUP
    index = row_index(x, core ^ (rel // 2), z ^ (rel % 2))
    return jnp.where(j < GROUP, index, 31 - index) * HALF


def list_kernel(meta_ref, list_ref):
    first_end, second_end = meta_ref[0], meta_ref[1]

    def queries(j, count):
        row = query_row_of(meta_ref, j)
        lowest = first_of(row, first_end, second_end)

        def keys(slot, count):
            key_row = key_row_of(meta_ref, slot)
            valid = (key_row <= row) & (key_row + HALF > lowest)
            list_ref[count] = j * 8 + slot
            return count + valid.astype(jnp.int32)

        return lax.fori_loop(0, 2 * GROUP, keys, count, unroll=True)

    count = lax.fori_loop(0, 2 * GROUP, queries, jnp.int32(0))
    list_ref[LIST - 1] = count


def sweep(meta_ref, list_ref, one, key_axis, size):
    def several(first, number):
        done = []
        for n in range(number):
            item = list_ref[first + n]
            j, slot = item // 8, item % 8
            rows, key_rows = query_row_of(meta_ref, j), key_row_of(meta_ref, slot)
            mask = mask_of(rows, key_rows, meta_ref[0], meta_ref[1], key_axis)
            done.append(one(j, slot, mask))
        for finish in done:
            finish()

    def step(i, carry):
        several(i * size, size)
        return carry

    def rest(i, carry):
        several(i, 1)
        return carry

    count = list_ref[LIST - 1]
    lax.fori_loop(0, count // size, step, 0)
    lax.fori_loop(count // size * size, count, rest, 0)


def mask_of(query_row, key_row, first_end, second_end, key_axis):
    shape_q = (HALF, 1) if key_axis == 1 else (1, HALF)
    rows_q = query_row + lax.broadcasted_iota(jnp.int32, shape_q, 1 - key_axis)
    rows_k = key_row + lax.broadcasted_iota(jnp.int32, (HALF, HALF), key_axis)
    return (rows_k <= rows_q) & (rows_k >= first_of(rows_q, first_end, second_end))


def forward_kernel(
    meta_ref, kv0, kv1, kv3, kv2, q0, q1, q2, q3, list_ref,
    keep_ref, send_ref, k_ref, v_ref, q_ref, acc,
):
    bucket = lax.broadcasted_iota(jnp.int32, (NB, HALF), 0).astype(F32)
    for rel, kv in enumerate((kv0, kv1, kv2, kv3)):
        tail = kv[ROWS : ROWS + 16, :].astype(F32)
        for half in (0, 1):
            rows = slice(half * HALF, (half + 1) * HALF)
            hot = (bucket == tail[half : half + 1, :]).astype(F32)
            k_ref[rel * 2 + half, :, 0:DH] = kv[rows, 0:DH]
            k_ref[rel * 2 + half, :, DH : 2 * DH] = hot.T.astype(BF)
            v_ref[rel * 2 + half] = kv[rows, DH : 2 * DH]
    for rel, q in enumerate((q0, q1, q2, q3)):
        for half in (0, 1):
            q_ref[half * GROUP + rel] = q[half * HALF : (half + 1) * HALF, :]
    acc[...] = jnp.zeros_like(acc)

    def one(j, slot, mask):
        scores = dot(q_ref[j], k_ref[slot], NT)
        attend = jnp.where(mask, scores + scores * jnp.tanh(scores), 0.0)
        result = dot(attend.astype(BF), v_ref[slot])

        def finish():
            acc[j] += result

        return finish

    sweep(meta_ref, list_ref, one, 1, 4)
    for rel in (0, 1):
        for half in (0, 1):
            rows = slice(rel * ROWS + half * HALF, rel * ROWS + (half + 1) * HALF)
            keep_ref[rows, :] = acc[half * GROUP + rel]
            send_ref[rows, :] = acc[half * GROUP + rel + 2].astype(BF)


def middle_kernel(
    meta_ref, keep, got_core, got_z, up0, up1, up2, up3, wout, gate, slope,
    grad_ref, gate_ref, gated_ref,
    grad_gated_ref, gated,
):
    y = meta_ref[5]
    for rel, up in enumerate((up0, up1, up2, up3)):
        rows = pl.ds(pl.multiple_of((y ^ rel) * DH, DH), DH)
        grad_gated_ref[rows, :] = dot(up[DH + 16 :, :], wout[...], NT)
    first_end, second_end, x, core, z = (meta_ref[n] for n in range(5))
    block = row_index(x, core, z)
    offset = lax.broadcasted_iota(jnp.int32, (ROWS, 1), 0)
    rows = jnp.where(offset < HALF, block * HALF + offset, (31 - block) * HALF + offset - HALF)
    first = jnp.where(rows < first_end, 0, jnp.where(rows < second_end, first_end, second_end))
    inverse = 1.0 / jnp.maximum(rows - first + 1, 1).astype(F32)
    total = keep[0:ROWS, :] + got_core[0:ROWS, :].astype(F32) + got_z[...].astype(F32)
    attended = total * inverse
    spread = 1.0 / jnp.sqrt(jnp.mean(attended * attended, axis=-1, keepdims=True) + EPSILON)
    normed = attended * spread
    gate_float = gate[...].astype(F32)
    gated[...] = (normed * gate_float).astype(BF)
    for rel in range(GROUP):
        rows = pl.ds(pl.multiple_of((y ^ rel) * DH, DH), DH)
        gated_ref[rel * DH : (rel + 1) * DH, :] = gated[rows, :]
    grad_gated = grad_gated_ref[...]
    gate_ref[...] = (grad_gated * normed * slope[:, 0:DH]).astype(BF)
    grad_normed = grad_gated * gate_float
    inner = jnp.mean(grad_normed * normed, axis=-1, keepdims=True)
    grad_ref[...] = ((grad_normed - normed * inner) * (spread * inverse * 0.5)).astype(BF)


def backward_kernel(
    meta_ref, list_ref, k_ref, v_ref, q_ref, g0, g1, g2, g3,
    own_ref, s1_ref, s2_ref, s3_ref, keep_ref, send_ref,
    grad, kt, acc_k, acc_v, acc_q,
):
    for rel, g in enumerate((g0, g1, g2, g3)):
        for half in (0, 1):
            grad[half * GROUP + rel] = g[half * HALF : (half + 1) * HALF, :]
    for slot in range(2 * GROUP):
        kt[slot] = k_ref[slot, :, 0:DH].astype(F32).T.astype(BF)
    acc_k[...] = jnp.zeros_like(acc_k)
    acc_v[...] = jnp.zeros_like(acc_v)
    acc_q[...] = jnp.zeros_like(acc_q)

    def one(j, slot, mask):
        scores = dot(k_ref[slot], q_ref[j], NT)
        raw = dot(v_ref[slot], grad[j], NT)
        tanh = jnp.tanh(scores)
        more = 1.0 + tanh
        attend = scores * more
        slope = jnp.where(mask, raw * (more + attend * (1.0 - tanh)), 0.0).astype(BF)
        attend = jnp.where(mask, attend, 0.0).astype(BF)
        grad_q = dot(kt[slot], slope)
        grad_k = dot(slope, q_ref[j, :, 0:DH])
        grad_v = dot(attend, grad[j])

        def finish():
            acc_q[j] += grad_q
            acc_k[slot] += grad_k
            acc_v[slot] += grad_v

        return finish

    sweep(meta_ref, list_ref, one, 0, 4)
    for rel, out in enumerate((own_ref, s1_ref, s2_ref, s3_ref)):
        for half in (0, 1):
            rows = slice(half * HALF, (half + 1) * HALF)
            out[rows, 0:DH] = (acc_k[rel * 2 + half] * 2.0).astype(out.dtype)
            out[rows, DH : 2 * DH] = (acc_v[rel * 2 + half] * 2.0).astype(out.dtype)
    for rel in (0, 1):
        for half in (0, 1):
            rows = slice(rel * ROWS + half * HALF, rel * ROWS + (half + 1) * HALF)
            keep_ref[rows, :] = acc_q[half * GROUP + rel].T * FACTOR
            send_ref[rows, :] = (acc_q[half * GROUP + rel + 2].T * FACTOR).astype(BF)


def wout_kernel(gated, up0, up1, up2, up3, out_ref):
    total = dot(gated[0:DH, :], up0[DH + 16 :, :], TN)
    for rel, up in ((1, up1), (2, up2), (3, up3)):
        total = total + dot(gated[rel * DH : (rel + 1) * DH, :], up[DH + 16 :, :], TN)
    out_ref[...] = total


def tail_kernel(
    meta_ref, own, r2, r1, r3, keep, got_core, got_z, grad_gate, slope, w, x_all, wout_terms,
    t0_ref, t1_ref, t2_ref, t3_ref, stay_ref, away_ref,
    grad, full,
):
    core, y = meta_ref[3], meta_ref[5]
    kv = own[...] + r1[...].astype(F32) + r2[...].astype(F32) + r3[...].astype(F32)
    query = keep[0:ROWS, :] + got_core[0:ROWS, :].astype(F32) + got_z[...].astype(F32)
    grad[:, 0:DH] = grad_gate[...]
    grad[:, DH : 2 * DH] = (kv[:, DH:] * slope[:, DH : 2 * DH]).astype(BF)
    grad[:, 2 * DH : 3 * DH] = (query * slope[:, 2 * DH : 3 * DH]).astype(BF)
    grad[:, 3 * DH :] = (kv[:, 0:DH] * slope[:, 3 * DH :]).astype(BF)
    for rel, out in enumerate((t0_ref, t1_ref, t2_ref, t3_ref)):
        rows = w[pl.ds(pl.multiple_of((y ^ rel) * DH, DH), DH), :]
        out[...] = dot(grad[...], rows, NT).astype(out.dtype)
    full[0:WIDTH, :] = dot(x_all[...], grad[...], TN)
    full[WIDTH:, :] = wout_terms[...]
    size = full.shape[0] // 2
    stay_ref[...] = full[pl.ds(pl.multiple_of(core * size, 64), size), :]
    away_ref[...] = full[pl.ds(pl.multiple_of((1 - core) * size, 64), size), :].astype(BF)


def sum_kernel(p0, p1, p2, p3, _, __, ___, total_ref, *passed):
    total = p0[...] + p1[...].astype(F32) + p2[...].astype(F32) + p3[...].astype(F32)
    total_ref[...] = total.astype(BF)


def both_kernel(a, b, t0, t1, t2, t3, total_ref, grad_ref):
    total_ref[...] = (a[...].astype(F32) + b[...].astype(F32)).astype(BF)
    grad = t0[...] + t1[...].astype(F32) + t2[...].astype(F32) + t3[...].astype(F32)
    grad_ref[...] = grad.astype(BF)


def split_kernel(meta_ref, stay, got, p0_ref, p1_ref, p2_ref, p3_ref, total):
    x = meta_ref[2]
    total[...] = stay[...] + got[...].astype(F32)
    for rel, out in enumerate((p0_ref, p1_ref, p2_ref, p3_ref)):
        rows = pl.ds(pl.multiple_of((x ^ rel) * PIECE, 16), PIECE)
        out[...] = total[rows, :].astype(out.dtype)


def join_kernel(meta_ref, p0, p1, p3, p2, _, out_ref):
    x = meta_ref[2]
    for rel, piece in enumerate((p0, p1, p2, p3)):
        out_ref[pl.ds(pl.multiple_of((x ^ rel) * PIECE, 16), PIECE), :] = piece[...]


def final_kernel(scale, meta_ref, mine, other, grad, win_ref, wout_ref, grad_ref):
    swapped = meta_ref[3] == 1
    size = mine.shape[0]
    low = jnp.where(swapped, other[...].astype(F32), mine[...].astype(F32)) * scale
    high = jnp.where(swapped, mine[...].astype(F32), other[...].astype(F32)) * scale
    win_ref[0:size, :] = low
    win_ref[size:, :] = high[0 : WIDTH - size, :]
    wout_ref[...] = high[WIDTH - size :, :]
    grad_ref[0] = grad[...]


def body(layer_input, grad_output, weight_in, weight_out, time_table, user_lengths, time_buckets):
    (xa,) = call(
        prepare_kernel,
        [((2 * DH + 16, WIDTH), BF)],
        (layer_input[0], time_buckets, user_lengths, grad_output[0]),
        held=4,
        limit=60,
        scratch=[
            pltpu.VMEM((1, ROWS), jnp.int32),
            pltpu.VMEM((1, 3), jnp.int32),
            pltpu.SemaphoreType.DMA((4,)),
        ],
    )
    xa = lax.ppermute(xa, MOVED, AWAY)

    flip_y = [[(i, i ^ rel) for i in range(4)] for rel in range(4)]
    x1, x3, x2 = (lax.ppermute(xa, "y", flip_y[rel]) for rel in (1, 3, 2))
    core = lax.axis_index("core")
    x = 2 * lax.axis_index("xh") + lax.axis_index("xl")
    z = lax.axis_index("z0")
    lengths = PAD_ROWS * xa[DH + 1, 0:2].astype(jnp.int32)
    places = jnp.stack([x, core, z, lax.axis_index("y"), 0 * x, 0 * x])
    meta = jnp.concatenate(
        [lengths[0:1], lengths[0:1] + lengths[1:2], places.astype(jnp.int32)]
    )

    (pairs,) = call(list_kernel, [((LIST,), jnp.int32)], (meta,))
    kv, q, gate, slope, x_all = call(
        project_kernel,
        [((ROWS + 16, 2 * DH), BF), ((ROWS, 2 * DH), BF), ((ROWS, DH), BF), ((ROWS, WIDTH), F32)]
        + [((ROWS, WIDTH), BF)],
        (pairs, xa, x1, x2, x3, weight_in, time_table),
        flops=2 * ROWS * WIDTH * WIDTH,
    )
    kvs = [kv] + [lax.ppermute(kv, ("xh", "xl"), flip_x(rel)) for rel in (1, 3, 2)]
    kvs = [kvs[0], kvs[1], kvs[3], kvs[2]]
    q_z = lax.ppermute(q, "z0", FLIP)
    qs = [q, q_z, lax.ppermute(q, "core", FLIP), lax.ppermute(q_z, "core", FLIP)]

    blocks = 2 * GROUP
    keep, send, k_all, v_all, q_all = call(
        forward_kernel,
        [
            ((2 * ROWS, DH), F32),
            ((2 * ROWS, DH), BF),
            ((blocks, HALF, 2 * DH), BF),
            ((blocks, HALF, DH), BF),
            ((blocks, HALF, 2 * DH), BF),
        ],
        (meta, kvs[0], kvs[1], kvs[3], kvs[2], *qs, pairs),
        scratch=[pltpu.VMEM((blocks, HALF, DH), F32)],
        flops=20 * 6 * HALF * HALF * DH,
    )
    got_core = lax.ppermute(send, "core", FLIP)
    part = (keep[ROWS:] + got_core[ROWS:].astype(F32)).astype(BF)
    got_z = lax.ppermute(part, "z0", FLIP)

    grad, grad_gate, gated = call(
        middle_kernel,
        [((ROWS, DH), BF)] * 3,
        (meta, keep, got_core, got_z, xa, x1, x2, x3, weight_out, gate, slope),
        scratch=[pltpu.VMEM((ROWS, DH), F32), pltpu.VMEM((ROWS, DH), BF)],
        flops=2 * ROWS * WIDTH * DH,
    )
    grad_z = lax.ppermute(grad, "z0", FLIP)
    grads = [grad, grad_z, lax.ppermute(grad, "core", FLIP), lax.ppermute(grad_z, "core", FLIP)]

    own, s1, s2, s3, keep, send = call(
        backward_kernel,
        [((ROWS, 2 * DH), F32)]
        + [((ROWS, 2 * DH), BF)] * 3
        + [((2 * ROWS, DH), F32), ((2 * ROWS, DH), BF)],
        (meta, pairs, k_all, v_all, q_all, *grads),
        scratch=[
            pltpu.VMEM((blocks, HALF, DH), BF),
            pltpu.VMEM((blocks, DH, HALF), BF),
            pltpu.VMEM((blocks, HALF, DH), F32),
            pltpu.VMEM((blocks, HALF, DH), F32),
            pltpu.VMEM((blocks, DH, HALF), F32),
        ],
        flops=20 * 12 * HALF * HALF * DH,
    )
    r1 = lax.ppermute(s1, ("xh", "xl"), flip_x(1))
    r3 = lax.ppermute(s3, ("xh", "xl"), flip_x(3))
    r2 = lax.ppermute(s2, ("xh", "xl"), flip_x(2))
    got_core = lax.ppermute(send, "core", FLIP)
    part = (keep[ROWS:] + got_core[ROWS:].astype(F32)).astype(BF)
    got_z = lax.ppermute(part, "z0", FLIP)
    (wout_terms,) = call(wout_kernel, [((DH, WIDTH), F32)], (gated, xa, x1, x2, x3))

    t0, t1, t2, t3, stay, away = call(
        tail_kernel,
        [((ROWS, DH), F32)] + [((ROWS, DH), BF)] * 3 + [((320, WIDTH), F32), ((320, WIDTH), BF)],
        (meta, own, r2, r1, r3, keep, got_core, got_z, grad_gate, slope, weight_in, x_all, wout_terms),
        scratch=[pltpu.VMEM((ROWS, WIDTH), BF), pltpu.VMEM((WIDTH + DH, WIDTH), F32)],
        flops=4 * ROWS * WIDTH * WIDTH,
    )
    got = lax.ppermute(away, "core", FLIP)
    p0, p1, p2, p3 = call(
        split_kernel,
        [((PIECE, WIDTH), F32)] + [((PIECE, WIDTH), BF)] * 3,
        (meta, stay, got),
        scratch=[pltpu.VMEM((GROUP * PIECE, WIDTH), F32)],
    )
    g1, g3, g2 = (
        lax.ppermute(p, ("xh", "xl"), flip_x(rel)) for p, rel in ((p1, 1), (p3, 3), (p2, 2))
    )
    total, t1, t2, t3 = call(
        sum_kernel, [((PIECE, WIDTH), BF)], (p0, g2, g1, g3, t1, t2, t3), passed=3
    )
    u1, u3, u2 = (lax.ppermute(t, "y", flip_y[rel]) for t, rel in ((t1, 1), (t3, 3), (t2, 2)))
    other = lax.ppermute(total, "z2", FLIP)
    total = (total.astype(F32) + other.astype(F32)).astype(BF)
    other = lax.ppermute(total, "z1", FLIP)
    total, grad_local = call(
        both_kernel,
        [((PIECE, WIDTH), BF), ((ROWS, DH), BF)],
        (total, other, t0, u1, u2, u3),
    )
    grad_local = lax.ppermute(grad_local, MOVED, HOME)
    other = lax.ppermute(total, "z0", FLIP)
    total = (total.astype(F32) + other.astype(F32)).astype(BF)
    h1, h3, h2 = (lax.ppermute(total, ("xh", "xl"), flip_x(rel)) for rel in (1, 3, 2))
    (mine_half,) = call(join_kernel, [((320, WIDTH), BF)], (meta, total, h1, h3, h2, grad_local), unread=1)
    other_half = lax.ppermute(mine_half, "core", FLIP)
    normalizer = 1.0 / math.sqrt(4 * 16 * ROWS)
    win, wout, grad_local = call(
        functools.partial(final_kernel, normalizer),
        [((WIDTH, WIDTH), F32), ((DH, WIDTH), F32), ((1, ROWS, DH), BF)],
        (meta, mine_half, other_half, grad_local),
    )
    return (grad_local, win, wout)


def solution(mesh):
    names = ("xh", "z2", "z1", "z0", "xl", "core", "y")
    fine = Mesh(mesh.devices.reshape(2, 2, 2, 2, 2, 2, 4), names)
    dp, seq = ("xl", "core"), ("xh", "z2", "z1", "z0")
    placed = (
        P(dp, seq, None),
        P(dp, seq, None),
        P(None, "y"),
        P("y", None),
        P("y", None),
        P(dp, None),
        P(dp, seq),
    )
    return jax.shard_map(
        body,
        mesh=fine,
        in_specs=placed,
        out_specs=(P(dp, seq, "y"), P(None, "y"), P("y", None)),
        check_vma=False,
    )
```

```python
import functools
import math

import jax
import jax.numpy as jnp
from jax import lax
from jax.experimental import pallas as pl
from jax.experimental.pallas import tpu as pltpu
from jax.sharding import Mesh
from jax.sharding import PartitionSpec as P

PAD_ROWS = 128
EPSILON = 0.05
ROWS = 512
HALF = 256
DH = 128
NB = 128
WIDTH = 512
GROUP = 4
BIG = 1 << 24
BF = jnp.bfloat16
F32 = jnp.float32
FACTOR = 1.0 / math.sqrt(DH)
PIECE = 80
LIST = 128

MOVED = ("z2", "z1", "z0", "xl", "core")
AWAY = [
    (16 * a + 8 * b + 4 * c + 2 * d + e, 16 * e + 8 * d + 4 * c + 2 * (b ^ c) + (a ^ b))
    for a in (0, 1)
    for b in (0, 1)
    for c in (0, 1)
    for d in (0, 1)
    for e in (0, 1)
]
HOME = [(b, a) for a, b in AWAY]
FLIP = [(0, 1), (1, 0)]


def flip_x(rel):
    return [(i, i ^ rel) for i in range(4)]


def row_index(x, core, z):
    middle = (x % 2) ^ z
    return 8 * (x // 2) + 4 * (core ^ middle) + 2 * middle + z


def dot(a, b, dims=((1,), (0,))):
    return lax.dot_general(a, b, (dims, ((), ())), preferred_element_type=F32)


NT = ((1,), (1,))
TN = ((0,), (0,))


def call(kernel, outs, args, scratch=(), flops=0, unread=0, passed=0, held=0, limit=40):
    specs = [pl.BlockSpec(memory_space=pltpu.VMEM)] * (len(args) - unread - passed)
    specs += [pl.BlockSpec(memory_space=pl.ANY)] * (unread + passed)
    specs[:held] = [pl.BlockSpec(memory_space=pltpu.HBM)] * held
    for n, a in enumerate(args):
        if a.ndim == 1:
            specs[n] = pl.BlockSpec(memory_space=pltpu.SMEM)
    before = len(outs)
    outs = list(outs) + [(a.shape, a.dtype) for a in args[len(args) - passed :]]
    out_specs = [pl.BlockSpec(memory_space=pltpu.VMEM)] * before
    out_specs += [pl.BlockSpec(memory_space=pl.ANY)] * passed
    for n, (shape, _) in enumerate(outs):
        if len(shape) == 1:
            out_specs[n] = pl.BlockSpec(memory_space=pltpu.SMEM)
    moved = sum(a.size * a.dtype.itemsize for a in args)
    moved += sum(math.prod(s) * jnp.dtype(t).itemsize for s, t in outs)
    return pl.pallas_call(
        kernel,
        out_shape=[jax.ShapeDtypeStruct(s, t) for s, t in outs],
        in_specs=specs,
        out_specs=out_specs,
        input_output_aliases={len(args) - passed + n: before + n for n in range(passed)},
        scratch_shapes=list(scratch),
        compiler_params=pltpu.CompilerParams(vmem_limit_bytes=limit * 1024 * 1024),
        cost_estimate=pl.CostEstimate(flops=flops, bytes_accessed=moved, transcendentals=0),
    )(*args)


def prepare_kernel(
    x_hbm, times_hbm, lengths_hbm, upstream_hbm, out_ref, times_ref, lengths_ref, sems
):
    quarter = pl.ds(pl.multiple_of(lax.axis_index("y") * DH, DH), DH)
    pairs = (
        (times_hbm, times_ref),
        (lengths_hbm, lengths_ref),
        (x_hbm.at[quarter, :], out_ref.at[0:DH, :]),
        (upstream_hbm.at[quarter, :], out_ref.at[DH + 16 :, :]),
    )
    copies = [pltpu.make_async_copy(a, b, sems.at[n]) for n, (a, b) in enumerate(pairs)]
    for copy in copies:
        copy.start()
    for copy in copies[:2]:
        copy.wait()
    row = lax.broadcasted_iota(jnp.int32, (16, WIDTH), 0)
    column = lax.broadcasted_iota(jnp.int32, (16, WIDTH), 1)
    lengths = lengths_ref[...].astype(F32)
    lengths = jnp.where(column == 0, lengths[:, 0:1], lengths[:, 1:2])
    times = times_ref[...].astype(F32)
    extra = jnp.where(row == 0, times, jnp.where(row == 1, lengths, 0.0))
    out_ref[DH : DH + 16, :] = extra.astype(BF)
    for copy in copies[2:]:
        copy.wait()


def project_kernel(
    _, xa_ref, x1, x2, x3, w_ref, table_ref, kv_ref, q_ref, gate_ref, slope_ref, x_ref
):
    y = lax.axis_index("y")
    for rel, piece in enumerate((xa_ref, x1, x2, x3)):
        x_ref[pl.ds(pl.multiple_of((y ^ rel) * DH, DH), DH), :] = piece[0:DH, :]
    projected = dot(x_ref[...], w_ref[...])
    sig = 0.5 + 0.5 * jnp.tanh(0.5 * projected)
    act = projected * sig
    slope_ref[...] = sig * (1.0 + projected * (1.0 - sig))
    gate_ref[...] = act[:, 0:DH].astype(BF)
    kv_ref[0:ROWS, DH : 2 * DH] = act[:, DH : 2 * DH].astype(BF)
    q_ref[:, 0:DH] = (act[:, 2 * DH : 3 * DH] * (0.5 * FACTOR)).astype(BF)
    kv_ref[0:ROWS, 0:DH] = act[:, 3 * DH : 4 * DH].astype(BF)
    times = xa_ref[DH : DH + 16, :].astype(F32)[0:1, :]
    row = lax.broadcasted_iota(jnp.int32, (16, HALF), 0)
    extra = jnp.where(row == 0, times[:, 0:HALF], jnp.where(row == 1, times[:, HALF:], 0.0))
    kv_ref[ROWS : ROWS + 16, :] = extra.astype(BF)
    table = jnp.broadcast_to(table_ref[...] * 0.5, (NB, NB))
    rolled = pltpu.roll(table, 0, 1, stride=1, stride_axis=0)
    first = lax.broadcasted_iota(jnp.int32, (NB, NB), 0)
    second = lax.broadcasted_iota(jnp.int32, (NB, NB), 1)
    square = jnp.where(second >= first, rolled, rolled.T).astype(BF)
    bucket = lax.broadcasted_iota(jnp.int32, (NB, ROWS), 0).astype(F32)
    hot = (bucket == times).astype(F32).astype(BF)
    q_ref[:, DH : 2 * DH] = dot(square, hot).T.astype(BF)


def first_of(rows, first_end, second_end):
    return jnp.where(rows < first_end, 0, jnp.where(rows < second_end, first_end, BIG))


def key_row_of(meta_ref, slot):
    x, core, z = (meta_ref[n] for n in range(2, 5))
    owner = x ^ (slot // 2)
    index = row_index(owner, core, z)
    return jnp.where(slot % 2 == 0, index, 31 - index) * HALF


def query_row_of(meta_ref, j):
    x, core, z = (meta_ref[n] for n in range(2, 5))
    rel = j % GROUP
    index = row_index(x, core ^ (rel // 2), z ^ (rel % 2))
    return jnp.where(j < GROUP, index, 31 - index) * HALF


def list_kernel(meta_ref, list_ref):
    first_end, second_end = meta_ref[0], meta_ref[1]

    def queries(j, count):
        row = query_row_of(meta_ref, j)
        lowest = first_of(row, first_end, second_end)

        def keys(slot, count):
            key_row = key_row_of(meta_ref, slot)
            valid = (key_row <= row) & (key_row + HALF > lowest)
            list_ref[count] = j * 8 + slot
            return count + valid.astype(jnp.int32)

        return lax.fori_loop(0, 2 * GROUP, keys, count, unroll=True)

    count = lax.fori_loop(0, 2 * GROUP, queries, jnp.int32(0))
    list_ref[LIST - 1] = count


def sweep(meta_ref, list_ref, one, key_axis, size):
    def several(first, number):
        done = []
        for n in range(number):
            item = list_ref[first + n]
            j, slot = item // 8, item % 8
            rows, key_rows = query_row_of(meta_ref, j), key_row_of(meta_ref, slot)
            mask = mask_of(rows, key_rows, meta_ref[0], meta_ref[1], key_axis)
            done.append(one(j, slot, mask))
        for finish in done:
            finish()

    def step(i, carry):
        several(i * size, size)
        return carry

    def rest(i, carry):
        several(i, 1)
        return carry

    count = list_ref[LIST - 1]
    lax.fori_loop(0, count // size, step, 0)
    lax.fori_loop(count // size * size, count, rest, 0)


def mask_of(query_row, key_row, first_end, second_end, key_axis):
    shape_q = (HALF, 1) if key_axis == 1 else (1, HALF)
    rows_q = query_row + lax.broadcasted_iota(jnp.int32, shape_q, 1 - key_axis)
    rows_k = key_row + lax.broadcasted_iota(jnp.int32, (HALF, HALF), key_axis)
    return (rows_k <= rows_q) & (rows_k >= first_of(rows_q, first_end, second_end))


def forward_kernel(
    meta_ref, kv0, kv1, kv3, kv2, q0, q1, q2, q3, list_ref,
    keep_ref, send_ref, k_ref, v_ref, q_ref, acc,
):
    bucket = lax.broadcasted_iota(jnp.int32, (NB, HALF), 0).astype(F32)
    for rel, kv in enumerate((kv0, kv1, kv2, kv3)):
        tail = kv[ROWS : ROWS + 16, :].astype(F32)
        for half in (0, 1):
            rows = slice(half * HALF, (half + 1) * HALF)
            hot = (bucket == tail[half : half + 1, :]).astype(F32)
            k_ref[rel * 2 + half, :, 0:DH] = kv[rows, 0:DH]
            k_ref[rel * 2 + half, :, DH : 2 * DH] = hot.T.astype(BF)
            v_ref[rel * 2 + half] = kv[rows, DH : 2 * DH]
    for rel, q in enumerate((q0, q1, q2, q3)):
        for half in (0, 1):
            q_ref[half * GROUP + rel] = q[half * HALF : (half + 1) * HALF, :]
    acc[...] = jnp.zeros_like(acc)

    def one(j, slot, mask):
        scores = dot(q_ref[j], k_ref[slot], NT)
        attend = jnp.where(mask, scores + scores * jnp.tanh(scores), 0.0)
        result = dot(attend.astype(BF), v_ref[slot])

        def finish():
            acc[j] += result

        return finish

    sweep(meta_ref, list_ref, one, 1, 4)
    for rel in (0, 1):
        for half in (0, 1):
            rows = slice(rel * ROWS + half * HALF, rel * ROWS + (half + 1) * HALF)
            keep_ref[rows, :] = acc[half * GROUP + rel]
            send_ref[rows, :] = acc[half * GROUP + rel + 2].astype(BF)


def middle_kernel(
    meta_ref, keep, got_core, got_z, up0, up1, up2, up3, wout, gate, slope,
    grad_ref, gate_ref, gated_ref,
    grad_gated_ref, gated,
):
    y = meta_ref[5]
    for rel, up in enumerate((up0, up1, up2, up3)):
        rows = pl.ds(pl.multiple_of((y ^ rel) * DH, DH), DH)
        grad_gated_ref[rows, :] = dot(up[DH + 16 :, :], wout[...], NT)
    first_end, second_end, x, core, z = (meta_ref[n] for n in range(5))
    block = row_index(x, core, z)
    offset = lax.broadcasted_iota(jnp.int32, (ROWS, 1), 0)
    rows = jnp.where(offset < HALF, block * HALF + offset, (31 - block) * HALF + offset - HALF)
    first = jnp.where(rows < first_end, 0, jnp.where(rows < second_end, first_end, second_end))
    inverse = 1.0 / jnp.maximum(rows - first + 1, 1).astype(F32)
    total = keep[0:ROWS, :] + got_core[0:ROWS, :].astype(F32) + got_z[...].astype(F32)
    attended = total * inverse
    spread = 1.0 / jnp.sqrt(jnp.mean(attended * attended, axis=-1, keepdims=True) + EPSILON)
    normed = attended * spread
    gate_float = gate[...].astype(F32)
    gated[...] = (normed * gate_float).astype(BF)
    for rel in range(GROUP):
        rows = pl.ds(pl.multiple_of((y ^ rel) * DH, DH), DH)
        gated_ref[rel * DH : (rel + 1) * DH, :] = gated[rows, :]
    grad_gated = grad_gated_ref[...]
    gate_ref[...] = (grad_gated * normed * slope[:, 0:DH]).astype(BF)
    grad_normed = grad_gated * gate_float
    inner = jnp.mean(grad_normed * normed, axis=-1, keepdims=True)
    grad_ref[...] = ((grad_normed - normed * inner) * (spread * inverse * 0.5)).astype(BF)


def backward_kernel(
    meta_ref, list_ref, k_ref, v_ref, q_ref, g0, g1, g2, g3,
    own_ref, s1_ref, s2_ref, s3_ref, keep_ref, send_ref,
    grad, kt, acc_k, acc_v, acc_q,
):
    for rel, g in enumerate((g0, g1, g2, g3)):
        for half in (0, 1):
            grad[half * GROUP + rel] = g[half * HALF : (half + 1) * HALF, :]
    for slot in range(2 * GROUP):
        kt[slot] = k_ref[slot, :, 0:DH].astype(F32).T.astype(BF)
    acc_k[...] = jnp.zeros_like(acc_k)
    acc_v[...] = jnp.zeros_like(acc_v)
    acc_q[...] = jnp.zeros_like(acc_q)

    def one(j, slot, mask):
        scores = dot(k_ref[slot], q_ref[j], NT)
        raw = dot(v_ref[slot], grad[j], NT)
        tanh = jnp.tanh(scores)
        more = 1.0 + tanh
        attend = scores * more
        slope = jnp.where(mask, raw * (more + attend * (1.0 - tanh)), 0.0).astype(BF)
        attend = jnp.where(mask, attend, 0.0).astype(BF)
        grad_q = dot(kt[slot], slope)
        grad_k = dot(slope, q_ref[j, :, 0:DH])
        grad_v = dot(attend, grad[j])

        def finish():
            acc_q[j] += grad_q
            acc_k[slot] += grad_k
            acc_v[slot] += grad_v

        return finish

    sweep(meta_ref, list_ref, one, 0, 4)
    for rel, out in enumerate((own_ref, s1_ref, s2_ref, s3_ref)):
        for half in (0, 1):
            rows = slice(half * HALF, (half + 1) * HALF)
            out[rows, 0:DH] = (acc_k[rel * 2 + half] * 2.0).astype(out.dtype)
            out[rows, DH : 2 * DH] = (acc_v[rel * 2 + half] * 2.0).astype(out.dtype)
    for rel in (0, 1):
        for half in (0, 1):
            rows = slice(rel * ROWS + half * HALF, rel * ROWS + (half + 1) * HALF)
            keep_ref[rows, :] = acc_q[half * GROUP + rel].T * FACTOR
            send_ref[rows, :] = (acc_q[half * GROUP + rel + 2].T * FACTOR).astype(BF)


def wout_kernel(gated, up0, up1, up2, up3, out_ref):
    total = dot(gated[0:DH, :], up0[DH + 16 :, :], TN)
    for rel, up in ((1, up1), (2, up2), (3, up3)):
        total = total + dot(gated[rel * DH : (rel + 1) * DH, :], up[DH + 16 :, :], TN)
    out_ref[...] = total


def tail_kernel(
    meta_ref, own, r2, r1, r3, keep, got_core, got_z, grad_gate, slope, w, x_all, wout_terms,
    t0_ref, t1_ref, t2_ref, t3_ref, stay_ref, away_ref,
    grad, full,
):
    core, y = meta_ref[3], meta_ref[5]
    kv = own[...] + r1[...].astype(F32) + r2[...].astype(F32) + r3[...].astype(F32)
    query = keep[0:ROWS, :] + got_core[0:ROWS, :].astype(F32) + got_z[...].astype(F32)
    grad[:, 0:DH] = grad_gate[...]
    grad[:, DH : 2 * DH] = (kv[:, DH:] * slope[:, DH : 2 * DH]).astype(BF)
    grad[:, 2 * DH : 3 * DH] = (query * slope[:, 2 * DH : 3 * DH]).astype(BF)
    grad[:, 3 * DH :] = (kv[:, 0:DH] * slope[:, 3 * DH :]).astype(BF)
    for rel, out in enumerate((t0_ref, t1_ref, t2_ref, t3_ref)):
        rows = w[pl.ds(pl.multiple_of((y ^ rel) * DH, DH), DH), :]
        out[...] = dot(grad[...], rows, NT).astype(out.dtype)
    full[0:WIDTH, :] = dot(x_all[...], grad[...], TN)
    full[WIDTH:, :] = wout_terms[...]
    size = full.shape[0] // 2
    stay_ref[...] = full[pl.ds(pl.multiple_of(core * size, 64), size), :]
    away_ref[...] = full[pl.ds(pl.multiple_of((1 - core) * size, 64), size), :].astype(BF)


def sum_kernel(p0, p1, p2, p3, _, __, ___, total_ref, *passed):
    total = p0[...] + p1[...].astype(F32) + p2[...].astype(F32) + p3[...].astype(F32)
    total_ref[...] = total.astype(BF)


def both_kernel(a, b, t0, t1, t2, t3, total_ref, grad_ref):
    total_ref[...] = (a[...].astype(F32) + b[...].astype(F32)).astype(BF)
    grad = t0[...] + t1[...].astype(F32) + t2[...].astype(F32) + t3[...].astype(F32)
    grad_ref[...] = grad.astype(BF)


def add_kernel(a, b, _, out_ref, __):
    out_ref[...] = (a[...].astype(F32) + b[...].astype(F32)).astype(BF)


def split_kernel(meta_ref, stay, got, p0_ref, p1_ref, p2_ref, p3_ref, total):
    x = meta_ref[2]
    total[...] = stay[...] + got[...].astype(F32)
    for rel, out in enumerate((p0_ref, p1_ref, p2_ref, p3_ref)):
        rows = pl.ds(pl.multiple_of((x ^ rel) * PIECE, 16), PIECE)
        out[...] = total[rows, :].astype(out.dtype)


def join_kernel(meta_ref, p0, p1, p3, p2, out_ref):
    x = meta_ref[2]
    for rel, piece in enumerate((p0, p1, p2, p3)):
        out_ref[pl.ds(pl.multiple_of((x ^ rel) * PIECE, 16), PIECE), :] = piece[...]


def final_kernel(scale, meta_ref, mine, other, grad, win_ref, wout_ref, grad_ref):
    swapped = meta_ref[3] == 1
    size = mine.shape[0]
    low = jnp.where(swapped, other[...].astype(F32), mine[...].astype(F32)) * scale
    high = jnp.where(swapped, mine[...].astype(F32), other[...].astype(F32)) * scale
    win_ref[0:size, :] = low
    win_ref[size:, :] = high[0 : WIDTH - size, :]
    wout_ref[...] = high[WIDTH - size :, :]
    grad_ref[0] = grad[...]


def body(layer_input, grad_output, weight_in, weight_out, time_table, user_lengths, time_buckets):
    (xa,) = call(
        prepare_kernel,
        [((2 * DH + 16, WIDTH), BF)],
        (layer_input[0], time_buckets, user_lengths, grad_output[0]),
        held=4,
        limit=60,
        scratch=[
            pltpu.VMEM((1, ROWS), jnp.int32),
            pltpu.VMEM((1, 3), jnp.int32),
            pltpu.SemaphoreType.DMA((4,)),
        ],
    )
    xa = lax.ppermute(xa, MOVED, AWAY)

    flip_y = [[(i, i ^ rel) for i in range(4)] for rel in range(4)]
    x1, x3, x2 = (lax.ppermute(xa, "y", flip_y[rel]) for rel in (1, 3, 2))
    core = lax.axis_index("core")
    x = 2 * lax.axis_index("xh") + lax.axis_index("xl")
    z = lax.axis_index("z0")
    lengths = PAD_ROWS * xa[DH + 1, 0:2].astype(jnp.int32)
    places = jnp.stack([x, core, z, lax.axis_index("y"), 0 * x, 0 * x])
    meta = jnp.concatenate(
        [lengths[0:1], lengths[0:1] + lengths[1:2], places.astype(jnp.int32)]
    )

    (pairs,) = call(list_kernel, [((LIST,), jnp.int32)], (meta,))
    kv, q, gate, slope, x_all = call(
        project_kernel,
        [((ROWS + 16, 2 * DH), BF), ((ROWS, 2 * DH), BF), ((ROWS, DH), BF), ((ROWS, WIDTH), F32)]
        + [((ROWS, WIDTH), BF)],
        (pairs, xa, x1, x2, x3, weight_in, time_table),
        flops=2 * ROWS * WIDTH * WIDTH,
    )
    kvs = [kv] + [lax.ppermute(kv, ("xh", "xl"), flip_x(rel)) for rel in (1, 3, 2)]
    kvs = [kvs[0], kvs[1], kvs[3], kvs[2]]
    q_z = lax.ppermute(q, "z0", FLIP)
    qs = [q, q_z, lax.ppermute(q, "core", FLIP), lax.ppermute(q_z, "core", FLIP)]

    blocks = 2 * GROUP
    keep, send, k_all, v_all, q_all = call(
        forward_kernel,
        [
            ((2 * ROWS, DH), F32),
            ((2 * ROWS, DH), BF),
            ((blocks, HALF, 2 * DH), BF),
            ((blocks, HALF, DH), BF),
            ((blocks, HALF, 2 * DH), BF),
        ],
        (meta, kvs[0], kvs[1], kvs[3], kvs[2], *qs, pairs),
        scratch=[pltpu.VMEM((blocks, HALF, DH), F32)],
        flops=20 * 6 * HALF * HALF * DH,
    )
    got_core = lax.ppermute(send, "core", FLIP)
    part = (keep[ROWS:] + got_core[ROWS:].astype(F32)).astype(BF)
    got_z = lax.ppermute(part, "z0", FLIP)

    grad, grad_gate, gated = call(
        middle_kernel,
        [((ROWS, DH), BF)] * 3,
        (meta, keep, got_core, got_z, xa, x1, x2, x3, weight_out, gate, slope),
        scratch=[pltpu.VMEM((ROWS, DH), F32), pltpu.VMEM((ROWS, DH), BF)],
        flops=2 * ROWS * WIDTH * DH,
    )
    grad_z = lax.ppermute(grad, "z0", FLIP)
    grads = [grad, grad_z, lax.ppermute(grad, "core", FLIP), lax.ppermute(grad_z, "core", FLIP)]

    own, s1, s2, s3, keep, send = call(
        backward_kernel,
        [((ROWS, 2 * DH), F32)]
        + [((ROWS, 2 * DH), BF)] * 3
        + [((2 * ROWS, DH), F32), ((2 * ROWS, DH), BF)],
        (meta, pairs, k_all, v_all, q_all, *grads),
        scratch=[
            pltpu.VMEM((blocks, HALF, DH), BF),
            pltpu.VMEM((blocks, DH, HALF), BF),
            pltpu.VMEM((blocks, HALF, DH), F32),
            pltpu.VMEM((blocks, HALF, DH), F32),
            pltpu.VMEM((blocks, DH, HALF), F32),
        ],
        flops=20 * 12 * HALF * HALF * DH,
    )
    r1 = lax.ppermute(s1, ("xh", "xl"), flip_x(1))
    r3 = lax.ppermute(s3, ("xh", "xl"), flip_x(3))
    r2 = lax.ppermute(s2, ("xh", "xl"), flip_x(2))
    got_core = lax.ppermute(send, "core", FLIP)
    part = (keep[ROWS:] + got_core[ROWS:].astype(F32)).astype(BF)
    got_z = lax.ppermute(part, "z0", FLIP)
    (wout_terms,) = call(wout_kernel, [((DH, WIDTH), F32)], (gated, xa, x1, x2, x3))

    t0, t1, t2, t3, stay, away = call(
        tail_kernel,
        [((ROWS, DH), F32)] + [((ROWS, DH), BF)] * 3 + [((320, WIDTH), F32), ((320, WIDTH), BF)],
        (meta, own, r2, r1, r3, keep, got_core, got_z, grad_gate, slope, weight_in, x_all, wout_terms),
        scratch=[pltpu.VMEM((ROWS, WIDTH), BF), pltpu.VMEM((WIDTH + DH, WIDTH), F32)],
        flops=4 * ROWS * WIDTH * WIDTH,
    )
    got = lax.ppermute(away, "core", FLIP)
    p0, p1, p2, p3 = call(
        split_kernel,
        [((PIECE, WIDTH), F32)] + [((PIECE, WIDTH), BF)] * 3,
        (meta, stay, got),
        scratch=[pltpu.VMEM((GROUP * PIECE, WIDTH), F32)],
    )
    g1, g3, g2 = (
        lax.ppermute(p, ("xh", "xl"), flip_x(rel)) for p, rel in ((p1, 1), (p3, 3), (p2, 2))
    )
    total, t1, t2, t3 = call(
        sum_kernel, [((PIECE, WIDTH), BF)], (p0, g2, g1, g3, t1, t2, t3), passed=3
    )
    u1, u3, u2 = (lax.ppermute(t, "y", flip_y[rel]) for t, rel in ((t1, 1), (t3, 3), (t2, 2)))
    other = lax.ppermute(total, "z2", FLIP)
    total = (total.astype(F32) + other.astype(F32)).astype(BF)
    other = lax.ppermute(total, "z1", FLIP)
    total, grad_local = call(
        both_kernel,
        [((PIECE, WIDTH), BF), ((ROWS, DH), BF)],
        (total, other, t0, u1, u2, u3),
    )
    other = lax.ppermute(total, "z0", FLIP)
    total, grad_local = call(
        add_kernel, [((PIECE, WIDTH), BF)], (total, other, grad_local), passed=1
    )
    grad_local = lax.ppermute(grad_local, MOVED, HOME)
    h1, h3, h2 = (lax.ppermute(total, ("xh", "xl"), flip_x(rel)) for rel in (1, 3, 2))
    (mine_half,) = call(join_kernel, [((320, WIDTH), BF)], (meta, total, h1, h3, h2))
    other_half = lax.ppermute(mine_half, "core", FLIP)
    normalizer = 1.0 / math.sqrt(4 * 16 * ROWS)
    win, wout, grad_local = call(
        functools.partial(final_kernel, normalizer),
        [((WIDTH, WIDTH), F32), ((DH, WIDTH), F32), ((1, ROWS, DH), BF)],
        (meta, mine_half, other_half, grad_local),
    )
    return (grad_local, win, wout)


def solution(mesh):
    names = ("xh", "z2", "z1", "z0", "xl", "core", "y")
    fine = Mesh(mesh.devices.reshape(2, 2, 2, 2, 2, 2, 4), names)
    dp, seq = ("xl", "core"), ("xh", "z2", "z1", "z0")
    placed = (
        P(dp, seq, None),
        P(dp, seq, None),
        P(None, "y"),
        P("y", None),
        P("y", None),
        P(dp, None),
        P(dp, seq),
    )
    return jax.shard_map(
        body,
        mesh=fine,
        in_specs=placed,
        out_specs=(P(dp, seq, "y"), P(None, "y"), P("y", None)),
        check_vma=False,
    )
```

```python
import functools
import math

import jax
import jax.numpy as jnp
from jax import lax
from jax.experimental import pallas as pl
from jax.experimental.pallas import tpu as pltpu
from jax.sharding import Mesh
from jax.sharding import PartitionSpec as P

PAD_ROWS = 128
EPSILON = 0.05
ROWS = 512
HALF = 256
DH = 128
NB = 128
WIDTH = 512
GROUP = 4
BIG = 1 << 24
BF = jnp.bfloat16
F32 = jnp.float32
FACTOR = 1.0 / math.sqrt(DH)
PIECE = 80
LIST = 128

MOVED = ("z2", "z1", "z0", "xl", "core")
AWAY = [
    (16 * a + 8 * b + 4 * c + 2 * d + e, 16 * e + 8 * d + 4 * c + 2 * (b ^ c) + (a ^ b))
    for a in (0, 1)
    for b in (0, 1)
    for c in (0, 1)
    for d in (0, 1)
    for e in (0, 1)
]
HOME = [(b, a) for a, b in AWAY]
FLIP = [(0, 1), (1, 0)]


def flip_x(rel):
    return [(i, i ^ rel) for i in range(4)]


def row_index(x, core, z):
    middle = (x % 2) ^ z
    return 8 * (x // 2) + 4 * (core ^ middle) + 2 * middle + z


def dot(a, b, dims=((1,), (0,))):
    return lax.dot_general(a, b, (dims, ((), ())), preferred_element_type=F32)


NT = ((1,), (1,))
TN = ((0,), (0,))


def call(kernel, outs, args, scratch=(), flops=0, unread=0, passed=0, held=0, limit=40):
    specs = [pl.BlockSpec(memory_space=pltpu.VMEM)] * (len(args) - unread - passed)
    specs += [pl.BlockSpec(memory_space=pl.ANY)] * (unread + passed)
    specs[:held] = [pl.BlockSpec(memory_space=pltpu.HBM)] * held
    for n, a in enumerate(args):
        if a.ndim == 1:
            specs[n] = pl.BlockSpec(memory_space=pltpu.SMEM)
    before = len(outs)
    outs = list(outs) + [(a.shape, a.dtype) for a in args[len(args) - passed :]]
    out_specs = [pl.BlockSpec(memory_space=pltpu.VMEM)] * before
    out_specs += [pl.BlockSpec(memory_space=pl.ANY)] * passed
    for n, (shape, _) in enumerate(outs):
        if len(shape) == 1:
            out_specs[n] = pl.BlockSpec(memory_space=pltpu.SMEM)
    moved = sum(a.size * a.dtype.itemsize for a in args)
    moved += sum(math.prod(s) * jnp.dtype(t).itemsize for s, t in outs)
    return pl.pallas_call(
        kernel,
        out_shape=[jax.ShapeDtypeStruct(s, t) for s, t in outs],
        in_specs=specs,
        out_specs=out_specs,
        input_output_aliases={len(args) - passed + n: before + n for n in range(passed)},
        scratch_shapes=list(scratch),
        compiler_params=pltpu.CompilerParams(vmem_limit_bytes=limit * 1024 * 1024),
        cost_estimate=pl.CostEstimate(flops=flops, bytes_accessed=moved, transcendentals=0),
    )(*args)


def prepare_kernel(
    x_hbm, times_hbm, lengths_hbm, upstream_hbm, out_ref, times_ref, lengths_ref, sems
):
    quarter = pl.ds(pl.multiple_of(lax.axis_index("y") * DH, DH), DH)
    pairs = (
        (times_hbm, times_ref),
        (lengths_hbm, lengths_ref),
        (x_hbm.at[quarter, :], out_ref.at[0:DH, :]),
        (upstream_hbm.at[quarter, :], out_ref.at[DH + 16 :, :]),
    )
    copies = [pltpu.make_async_copy(a, b, sems.at[n]) for n, (a, b) in enumerate(pairs)]
    for copy in copies:
        copy.start()
    for copy in copies[:2]:
        copy.wait()
    row = lax.broadcasted_iota(jnp.int32, (16, WIDTH), 0)
    column = lax.broadcasted_iota(jnp.int32, (16, WIDTH), 1)
    lengths = lengths_ref[...].astype(F32)
    lengths = jnp.where(column == 0, lengths[:, 0:1], lengths[:, 1:2])
    times = times_ref[...].astype(F32)
    extra = jnp.where(row == 0, times, jnp.where(row == 1, lengths, 0.0))
    out_ref[DH : DH + 16, :] = extra.astype(BF)
    for copy in copies[2:]:
        copy.wait()


def project_kernel(
    _, xa_ref, x1, x2, x3, w_ref, table_ref, kv_ref, q_ref, gate_ref, slope_ref, x_ref
):
    y = lax.axis_index("y")
    for rel, piece in enumerate((xa_ref, x1, x2, x3)):
        x_ref[pl.ds(pl.multiple_of((y ^ rel) * DH, DH), DH), :] = piece[0:DH, :]
    projected = dot(x_ref[...], w_ref[...])
    sig = 0.5 + 0.5 * jnp.tanh(0.5 * projected)
    act = projected * sig
    slope_ref[...] = sig * (1.0 + projected * (1.0 - sig))
    gate_ref[...] = act[:, 0:DH].astype(BF)
    kv_ref[0:ROWS, DH : 2 * DH] = act[:, DH : 2 * DH].astype(BF)
    q_ref[:, 0:DH] = (act[:, 2 * DH : 3 * DH] * (0.5 * FACTOR)).astype(BF)
    kv_ref[0:ROWS, 0:DH] = act[:, 3 * DH : 4 * DH].astype(BF)
    times = xa_ref[DH : DH + 16, :].astype(F32)[0:1, :]
    row = lax.broadcasted_iota(jnp.int32, (16, HALF), 0)
    extra = jnp.where(row == 0, times[:, 0:HALF], jnp.where(row == 1, times[:, HALF:], 0.0))
    kv_ref[ROWS : ROWS + 16, :] = extra.astype(BF)
    table = jnp.broadcast_to(table_ref[...] * 0.5, (NB, NB))
    rolled = pltpu.roll(table, 0, 1, stride=1, stride_axis=0)
    first = lax.broadcasted_iota(jnp.int32, (NB, NB), 0)
    second = lax.broadcasted_iota(jnp.int32, (NB, NB), 1)
    square = jnp.where(second >= first, rolled, rolled.T).astype(BF)
    bucket = lax.broadcasted_iota(jnp.int32, (NB, ROWS), 0).astype(F32)
    hot = (bucket == times).astype(F32).astype(BF)
    q_ref[:, DH : 2 * DH] = dot(square, hot).T.astype(BF)


def first_of(rows, first_end, second_end):
    return jnp.where(rows < first_end, 0, jnp.where(rows < second_end, first_end, BIG))


def key_row_of(meta_ref, slot):
    x, core, z = (meta_ref[n] for n in range(2, 5))
    owner = x ^ (slot // 2)
    index = row_index(owner, core, z)
    return jnp.where(slot % 2 == 0, index, 31 - index) * HALF


def query_row_of(meta_ref, j):
    x, core, z = (meta_ref[n] for n in range(2, 5))
    rel = j % GROUP
    index = row_index(x, core ^ (rel // 2), z ^ (rel % 2))
    return jnp.where(j < GROUP, index, 31 - index) * HALF


def list_kernel(meta_ref, list_ref):
    first_end, second_end = meta_ref[0], meta_ref[1]

    def queries(j, count):
        row = query_row_of(meta_ref, j)
        lowest = first_of(row, first_end, second_end)

        def keys(slot, count):
            key_row = key_row_of(meta_ref, slot)
            valid = (key_row <= row) & (key_row + HALF > lowest)
            list_ref[count] = j * 8 + slot
            return count + valid.astype(jnp.int32)

        return lax.fori_loop(0, 2 * GROUP, keys, count, unroll=True)

    count = lax.fori_loop(0, 2 * GROUP, queries, jnp.int32(0))
    list_ref[LIST - 1] = count


def sweep(meta_ref, list_ref, one, key_axis, size):
    def several(first, number):
        done = []
        for n in range(number):
            item = list_ref[first + n]
            j, slot = item // 8, item % 8
            rows, key_rows = query_row_of(meta_ref, j), key_row_of(meta_ref, slot)
            mask = mask_of(rows, key_rows, meta_ref[0], meta_ref[1], key_axis)
            done.append(one(j, slot, mask))
        for finish in done:
            finish()

    def step(i, carry):
        several(i * size, size)
        return carry

    def rest(i, carry):
        several(i, 1)
        return carry

    count = list_ref[LIST - 1]
    lax.fori_loop(0, count // size, step, 0)
    lax.fori_loop(count // size * size, count, rest, 0)


def mask_of(query_row, key_row, first_end, second_end, key_axis):
    shape_q = (HALF, 1) if key_axis == 1 else (1, HALF)
    rows_q = query_row + lax.broadcasted_iota(jnp.int32, shape_q, 1 - key_axis)
    rows_k = key_row + lax.broadcasted_iota(jnp.int32, (HALF, HALF), key_axis)
    return (rows_k <= rows_q) & (rows_k >= first_of(rows_q, first_end, second_end))


def forward_kernel(
    meta_ref, kv0, kv1, kv3, kv2, q0, q1, q2, q3, list_ref,
    keep_ref, send_ref, k_ref, v_ref, q_ref, acc,
):
    bucket = lax.broadcasted_iota(jnp.int32, (NB, HALF), 0).astype(F32)
    for rel, kv in enumerate((kv0, kv1, kv2, kv3)):
        tail = kv[ROWS : ROWS + 16, :].astype(F32)
        for half in (0, 1):
            rows = slice(half * HALF, (half + 1) * HALF)
            hot = (bucket == tail[half : half + 1, :]).astype(F32)
            k_ref[rel * 2 + half, :, 0:DH] = kv[rows, 0:DH]
            k_ref[rel * 2 + half, :, DH : 2 * DH] = hot.T.astype(BF)
            v_ref[rel * 2 + half] = kv[rows, DH : 2 * DH]
    for rel, q in enumerate((q0, q1, q2, q3)):
        for half in (0, 1):
            q_ref[half * GROUP + rel] = q[half * HALF : (half + 1) * HALF, :]
    acc[...] = jnp.zeros_like(acc)

    def one(j, slot, mask):
        scores = dot(q_ref[j], k_ref[slot], NT)
        attend = jnp.where(mask, scores + scores * jnp.tanh(scores), 0.0)
        result = dot(attend.astype(BF), v_ref[slot])

        def finish():
            acc[j] += result

        return finish

    sweep(meta_ref, list_ref, one, 1, 4)
    for rel in (0, 1):
        for half in (0, 1):
            rows = slice(rel * ROWS + half * HALF, rel * ROWS + (half + 1) * HALF)
            keep_ref[rows, :] = acc[half * GROUP + rel]
            send_ref[rows, :] = acc[half * GROUP + rel + 2].astype(BF)


def middle_kernel(
    meta_ref, keep, got_core, got_z, up0, up1, up2, up3, wout, gate, slope,
    grad_ref, gate_ref, gated_ref,
    grad_gated_ref, gated,
):
    y = meta_ref[5]
    for rel, up in enumerate((up0, up1, up2, up3)):
        rows = pl.ds(pl.multiple_of((y ^ rel) * DH, DH), DH)
        grad_gated_ref[rows, :] = dot(up[DH + 16 :, :], wout[...], NT)
    first_end, second_end, x, core, z = (meta_ref[n] for n in range(5))
    block = row_index(x, core, z)
    offset = lax.broadcasted_iota(jnp.int32, (ROWS, 1), 0)
    rows = jnp.where(offset < HALF, block * HALF + offset, (31 - block) * HALF + offset - HALF)
    first = jnp.where(rows < first_end, 0, jnp.where(rows < second_end, first_end, second_end))
    inverse = 1.0 / jnp.maximum(rows - first + 1, 1).astype(F32)
    total = keep[0:ROWS, :] + got_core[0:ROWS, :].astype(F32) + got_z[...].astype(F32)
    attended = total * inverse
    spread = 1.0 / jnp.sqrt(jnp.mean(attended * attended, axis=-1, keepdims=True) + EPSILON)
    normed = attended * spread
    gate_float = gate[...].astype(F32)
    gated[...] = (normed * gate_float).astype(BF)
    for rel in range(GROUP):
        rows = pl.ds(pl.multiple_of((y ^ rel) * DH, DH), DH)
        gated_ref[rel * DH : (rel + 1) * DH, :] = gated[rows, :]
    grad_gated = grad_gated_ref[...]
    gate_ref[...] = (grad_gated * normed * slope[:, 0:DH]).astype(BF)
    grad_normed = grad_gated * gate_float
    inner = jnp.mean(grad_normed * normed, axis=-1, keepdims=True)
    grad_ref[...] = ((grad_normed - normed * inner) * (spread * inverse * 0.5)).astype(BF)


def backward_kernel(
    meta_ref, list_ref, k_ref, v_ref, q_ref, g0, g1, g2, g3,
    own_ref, s1_ref, s2_ref, s3_ref, keep_ref, send_ref,
    grad, kt, acc_k, acc_v, acc_q,
):
    for rel, g in enumerate((g0, g1, g2, g3)):
        for half in (0, 1):
            grad[half * GROUP + rel] = g[half * HALF : (half + 1) * HALF, :]
    for slot in range(2 * GROUP):
        kt[slot] = k_ref[slot, :, 0:DH].astype(F32).T.astype(BF)
    acc_k[...] = jnp.zeros_like(acc_k)
    acc_v[...] = jnp.zeros_like(acc_v)
    acc_q[...] = jnp.zeros_like(acc_q)

    def one(j, slot, mask):
        scores = dot(k_ref[slot], q_ref[j], NT)
        raw = dot(v_ref[slot], grad[j], NT)
        tanh = jnp.tanh(scores)
        more = 1.0 + tanh
        attend = scores * more
        slope = jnp.where(mask, raw * (more + attend * (1.0 - tanh)), 0.0).astype(BF)
        attend = jnp.where(mask, attend, 0.0).astype(BF)
        grad_q = dot(kt[slot], slope)
        grad_k = dot(slope, q_ref[j, :, 0:DH])
        grad_v = dot(attend, grad[j])

        def finish():
            acc_q[j] += grad_q
            acc_k[slot] += grad_k
            acc_v[slot] += grad_v

        return finish

    sweep(meta_ref, list_ref, one, 0, 4)
    for rel, out in enumerate((own_ref, s1_ref, s2_ref, s3_ref)):
        for half in (0, 1):
            rows = slice(half * HALF, (half + 1) * HALF)
            out[rows, 0:DH] = (acc_k[rel * 2 + half] * 2.0).astype(out.dtype)
            out[rows, DH : 2 * DH] = (acc_v[rel * 2 + half] * 2.0).astype(out.dtype)
    for rel in (0, 1):
        for half in (0, 1):
            rows = slice(rel * ROWS + half * HALF, rel * ROWS + (half + 1) * HALF)
            keep_ref[rows, :] = acc_q[half * GROUP + rel].T * FACTOR
            send_ref[rows, :] = (acc_q[half * GROUP + rel + 2].T * FACTOR).astype(BF)


def wout_kernel(gated, up0, up1, up2, up3, out_ref):
    total = dot(gated[0:DH, :], up0[DH + 16 :, :], TN)
    for rel, up in ((1, up1), (2, up2), (3, up3)):
        total = total + dot(gated[rel * DH : (rel + 1) * DH, :], up[DH + 16 :, :], TN)
    out_ref[...] = total


def tail_kernel(
    meta_ref, own, r2, r1, r3, keep, got_core, got_z, grad_gate, slope, w, x_all, wout_terms,
    t0_ref, t1_ref, t2_ref, t3_ref, stay_ref, away_ref,
    grad, full,
):
    core, y = meta_ref[3], meta_ref[5]
    kv = own[...] + r1[...].astype(F32) + r2[...].astype(F32) + r3[...].astype(F32)
    query = keep[0:ROWS, :] + got_core[0:ROWS, :].astype(F32) + got_z[...].astype(F32)
    grad[:, 0:DH] = grad_gate[...]
    grad[:, DH : 2 * DH] = (kv[:, DH:] * slope[:, DH : 2 * DH]).astype(BF)
    grad[:, 2 * DH : 3 * DH] = (query * slope[:, 2 * DH : 3 * DH]).astype(BF)
    grad[:, 3 * DH :] = (kv[:, 0:DH] * slope[:, 3 * DH :]).astype(BF)
    for rel, out in enumerate((t0_ref, t1_ref, t2_ref, t3_ref)):
        rows = w[pl.ds(pl.multiple_of((y ^ rel) * DH, DH), DH), :]
        out[...] = dot(grad[...], rows, NT).astype(out.dtype)
    full[0:WIDTH, :] = dot(x_all[...], grad[...], TN)
    full[WIDTH:, :] = wout_terms[...]
    size = full.shape[0] // 2
    stay_ref[...] = full[pl.ds(pl.multiple_of(core * size, 64), size), :]
    away_ref[...] = full[pl.ds(pl.multiple_of((1 - core) * size, 64), size), :].astype(BF)


def sum_kernel(p0, p1, p2, p3, _, __, ___, total_ref, *passed):
    total = p0[...] + p1[...].astype(F32) + p2[...].astype(F32) + p3[...].astype(F32)
    total_ref[...] = total.astype(BF)


def both_kernel(a, b, t0, t1, t2, t3, total_ref, grad_ref):
    total_ref[...] = (a[...].astype(F32) + b[...].astype(F32)).astype(BF)
    grad = t0[...] + t1[...].astype(F32) + t2[...].astype(F32) + t3[...].astype(F32)
    grad_ref[...] = grad.astype(BF)


def split_kernel(meta_ref, stay, got, p0_ref, p1_ref, p2_ref, p3_ref, total):
    x = meta_ref[2]
    total[...] = stay[...] + got[...].astype(F32)
    for rel, out in enumerate((p0_ref, p1_ref, p2_ref, p3_ref)):
        rows = pl.ds(pl.multiple_of((x ^ rel) * PIECE, 16), PIECE)
        out[...] = total[rows, :].astype(out.dtype)


def join_kernel(meta_ref, p0, p1, p3, p2, _, out_ref):
    x = meta_ref[2]
    for rel, piece in enumerate((p0, p1, p2, p3)):
        out_ref[pl.ds(pl.multiple_of((x ^ rel) * PIECE, 16), PIECE), :] = piece[...]


def final_kernel(scale, meta_ref, mine, other, grad, win_ref, wout_ref, grad_ref):
    swapped = meta_ref[3] == 1
    size = mine.shape[0]
    low = jnp.where(swapped, other[...].astype(F32), mine[...].astype(F32)) * scale
    high = jnp.where(swapped, mine[...].astype(F32), other[...].astype(F32)) * scale
    win_ref[0:size, :] = low
    win_ref[size:, :] = high[0 : WIDTH - size, :]
    wout_ref[...] = high[WIDTH - size :, :]
    grad_ref[0] = grad[...]


def body(layer_input, grad_output, weight_in, weight_out, time_table, user_lengths, time_buckets):
    (xa,) = call(
        prepare_kernel,
        [((2 * DH + 16, WIDTH), BF)],
        (layer_input[0], time_buckets, user_lengths, grad_output[0]),
        held=4,
        limit=60,
        scratch=[
            pltpu.VMEM((1, ROWS), jnp.int32),
            pltpu.VMEM((1, 3), jnp.int32),
            pltpu.SemaphoreType.DMA((4,)),
        ],
    )
    xa = lax.ppermute(xa, MOVED, AWAY)

    flip_y = [[(i, i ^ rel) for i in range(4)] for rel in range(4)]
    x1, x3, x2 = (lax.ppermute(xa, "y", flip_y[rel]) for rel in (1, 3, 2))
    core = lax.axis_index("core")
    x = 2 * lax.axis_index("xh") + lax.axis_index("xl")
    z = lax.axis_index("z0")
    lengths = PAD_ROWS * xa[DH + 1, 0:2].astype(jnp.int32)
    places = jnp.stack([x, core, z, lax.axis_index("y"), 0 * x, 0 * x])
    meta = jnp.concatenate(
        [lengths[0:1], lengths[0:1] + lengths[1:2], places.astype(jnp.int32)]
    )

    (pairs,) = call(list_kernel, [((LIST,), jnp.int32)], (meta,))
    kv, q, gate, slope, x_all = call(
        project_kernel,
        [((ROWS + 16, 2 * DH), BF), ((ROWS, 2 * DH), BF), ((ROWS, DH), BF), ((ROWS, WIDTH), F32)]
        + [((ROWS, WIDTH), BF)],
        (pairs, xa, x1, x2, x3, weight_in, time_table),
        flops=2 * ROWS * WIDTH * WIDTH,
    )
    kvs = [kv] + [lax.ppermute(kv, ("xh", "xl"), flip_x(rel)) for rel in (1, 3, 2)]
    kvs = [kvs[0], kvs[1], kvs[3], kvs[2]]
    q_z = lax.ppermute(q, "z0", FLIP)
    qs = [q, q_z, lax.ppermute(q, "core", FLIP), lax.ppermute(q_z, "core", FLIP)]

    blocks = 2 * GROUP
    keep, send, k_all, v_all, q_all = call(
        forward_kernel,
        [
            ((2 * ROWS, DH), F32),
            ((2 * ROWS, DH), BF),
            ((blocks, HALF, 2 * DH), BF),
            ((blocks, HALF, DH), BF),
            ((blocks, HALF, 2 * DH), BF),
        ],
        (meta, kvs[0], kvs[1], kvs[3], kvs[2], *qs, pairs),
        scratch=[pltpu.VMEM((blocks, HALF, DH), F32)],
        flops=20 * 6 * HALF * HALF * DH,
    )
    got_core = lax.ppermute(send, "core", FLIP)
    part = (keep[ROWS:] + got_core[ROWS:].astype(F32)).astype(BF)
    got_z = lax.ppermute(part, "z0", FLIP)

    grad, grad_gate, gated = call(
        middle_kernel,
        [((ROWS, DH), BF)] * 3,
        (meta, keep, got_core, got_z, xa, x1, x2, x3, weight_out, gate, slope),
        scratch=[pltpu.VMEM((ROWS, DH), F32), pltpu.VMEM((ROWS, DH), BF)],
        flops=2 * ROWS * WIDTH * DH,
    )
    grad_z = lax.ppermute(grad, "z0", FLIP)
    grads = [grad, grad_z, lax.ppermute(grad, "core", FLIP), lax.ppermute(grad_z, "core", FLIP)]

    own, s1, s2, s3, keep, send = call(
        backward_kernel,
        [((ROWS, 2 * DH), F32)]
        + [((ROWS, 2 * DH), BF)] * 3
        + [((2 * ROWS, DH), F32), ((2 * ROWS, DH), BF)],
        (meta, pairs, k_all, v_all, q_all, *grads),
        scratch=[
            pltpu.VMEM((blocks, HALF, DH), BF),
            pltpu.VMEM((blocks, DH, HALF), BF),
            pltpu.VMEM((blocks, HALF, DH), F32),
            pltpu.VMEM((blocks, HALF, DH), F32),
            pltpu.VMEM((blocks, DH, HALF), F32),
        ],
        flops=20 * 12 * HALF * HALF * DH,
    )
    r1 = lax.ppermute(s1, ("xh", "xl"), flip_x(1))
    r3 = lax.ppermute(s3, ("xh", "xl"), flip_x(3))
    r2 = lax.ppermute(s2, ("xh", "xl"), flip_x(2))
    got_core = lax.ppermute(send, "core", FLIP)
    part = (keep[ROWS:] + got_core[ROWS:].astype(F32)).astype(BF)
    got_z = lax.ppermute(part, "z0", FLIP)
    (wout_terms,) = call(wout_kernel, [((DH, WIDTH), F32)], (gated, xa, x1, x2, x3))

    t0, t1, t2, t3, stay, away = call(
        tail_kernel,
        [((ROWS, DH), F32)] + [((ROWS, DH), BF)] * 3 + [((320, WIDTH), F32), ((320, WIDTH), BF)],
        (meta, own, r2, r1, r3, keep, got_core, got_z, grad_gate, slope, weight_in, x_all, wout_terms),
        scratch=[pltpu.VMEM((ROWS, WIDTH), BF), pltpu.VMEM((WIDTH + DH, WIDTH), F32)],
        flops=4 * ROWS * WIDTH * WIDTH,
    )
    got = lax.ppermute(away, "core", FLIP)
    p0, p1, p2, p3 = call(
        split_kernel,
        [((PIECE, WIDTH), F32)] + [((PIECE, WIDTH), BF)] * 3,
        (meta, stay, got),
        scratch=[pltpu.VMEM((GROUP * PIECE, WIDTH), F32)],
    )
    g1, g3, g2 = (
        lax.ppermute(p, ("xh", "xl"), flip_x(rel)) for p, rel in ((p1, 1), (p3, 3), (p2, 2))
    )
    total, t1, t2, t3 = call(
        sum_kernel, [((PIECE, WIDTH), BF)], (p0, g2, g1, g3, t1, t2, t3), passed=3
    )
    u1, u3, u2 = (lax.ppermute(t, "y", flip_y[rel]) for t, rel in ((t1, 1), (t3, 3), (t2, 2)))
    other = lax.ppermute(total, "z1", FLIP)
    total = (total.astype(F32) + other.astype(F32)).astype(BF)
    other = lax.ppermute(total, "z2", FLIP)
    total, grad_local = call(
        both_kernel,
        [((PIECE, WIDTH), BF), ((ROWS, DH), BF)],
        (total, other, t0, u1, u2, u3),
    )
    grad_local = lax.ppermute(grad_local, MOVED, HOME)
    other = lax.ppermute(total, "z0", FLIP)
    total = (total.astype(F32) + other.astype(F32)).astype(BF)
    h1, h3, h2 = (lax.ppermute(total, ("xh", "xl"), flip_x(rel)) for rel in (1, 3, 2))
    (mine_half,) = call(join_kernel, [((320, WIDTH), BF)], (meta, total, h1, h3, h2, grad_local), unread=1)
    other_half = lax.ppermute(mine_half, "core", FLIP)
    normalizer = 1.0 / math.sqrt(4 * 16 * ROWS)
    win, wout, grad_local = call(
        functools.partial(final_kernel, normalizer),
        [((WIDTH, WIDTH), F32), ((DH, WIDTH), F32), ((1, ROWS, DH), BF)],
        (meta, mine_half, other_half, grad_local),
    )
    return (grad_local, win, wout)


def solution(mesh):
    names = ("xh", "z2", "z1", "z0", "xl", "core", "y")
    fine = Mesh(mesh.devices.reshape(2, 2, 2, 2, 2, 2, 4), names)
    dp, seq = ("xl", "core"), ("xh", "z2", "z1", "z0")
    placed = (
        P(dp, seq, None),
        P(dp, seq, None),
        P(None, "y"),
        P("y", None),
        P("y", None),
        P(dp, None),
        P(dp, seq),
    )
    return jax.shard_map(
        body,
        mesh=fine,
        in_specs=placed,
        out_specs=(P(dp, seq, "y"), P(None, "y"), P("y", None)),
        check_vma=False,
    )
```
